32 devices in a mesh: dp: 8 (over z, core), row: 2 (over x), col: 2 (over y).
Axes of the slice: x: 2, y: 2, z: 4, core: 2. Of those that a mesh axis runs over, the one named last changes fastest.
Arguments:
- hidden_in: float32 [25088, 768], P(('dp', 'row', 'col')), may hold values from -6 to 6
- qkv_weight: bfloat16 [2, 2, 768, 3, 768], P(None, None, ('dp', 'row'), None, 'col'), may hold values from -0.21875 to 0.21875
- out_weight: bfloat16 [2, 2, 768, 768], P(None, None, 'col', ('dp', 'row')), may hold values from -0.625 to 0.625
- up_weight: bfloat16 [2, 768, 3072], P(None, ('dp', 'row'), 'col'), may hold values from -0.21875 to 0.21875
- down_weight: bfloat16 [2, 3072, 768], P(None, 'col', ('dp', 'row')), may hold values from -0.109375 to 0.109375
- qv_bias: float32 [2, 2, 2, 768], P(None, None, None, 'col'), may hold values from -3 to 3
- out_bias: float32 [2, 2, 768], replicated, may hold values from -3 to 3
- up_bias: float32 [2, 3072], P(None, 'col'), may hold values from -3 to 3
- down_bias: float32 [2, 768], replicated, may hold values from -3 to 3
- norm_gain: float32 [2, 3, 768], replicated, may hold values from 0.25 to 1.75
- norm_shift: float32 [2, 3, 768], replicated, may hold values from -2 to 2
- cotangent: float32 [25088, 768], P(('dp', 'row', 'col')), may hold values from -6 to 6
Outputs:
- hidden_out: float32 [25088, 768], P(('dp', 'row', 'col'))
- grad_in: float32 [25088, 768], P(('dp', 'row', 'col'))
- grad_qkv_weight: float32 [2, 2, 768, 3, 768], P(None, None, ('dp', 'row'), None, 'col')
- grad_out_weight: float32 [2, 2, 768, 768], P(None, None, 'col', ('dp', 'row'))
- grad_up_weight: float32 [2, 768, 3072], P(None, ('dp', 'row'), 'col')
- grad_down_weight: float32 [2, 3072, 768], P(None, 'col', ('dp', 'row'))
- grad_qv_bias: float32 [2, 2, 2, 768], P(None, None, None, 'col')
- grad_out_bias: float32 [2, 2, 768], replicated
- grad_up_bias: float32 [2, 3072], P(None, 'col')
- grad_down_bias: float32 [2, 768], replicated
- grad_norm_gain: float32 [2, 3, 768], replicated
- grad_norm_shift: float32 [2, 3, 768], replicated
The draws below stay inside these ranges and needn't reach their ends.
All inputs are finite; a program needn't handle non-finite values.
Results may differ from the reference program's by a relative error of at most 0.019.
Values may be sent and summed in bfloat16 or wider, within the bound.
No kernel may reach another device: no remote copies, remote signals or barrier semaphores. Data moves between devices by JAX's collectives and lax.ppermute only.
A program may use at most 320 MiB of HBM per device.

```python
import jax
import jax.numpy as jnp
from jax import lax

D = 768
FF = 3072
HEADS = 12
FRAMES = 16
PATCHES = 196
LAYERS = 2
CLIPS = 8
TOKENS = 25088


def spiked(values, rng, source, target, parts, factor):
    owner, partner = [(jnp.arange(values.shape[axis_at]) // (values.shape[axis_at] // parts)).reshape([-1 if axis == axis_at else 1 for axis in range(values.ndim)]) for axis_at in (source, target)]
    chosen = jax.random.permutation(rng, parts)[partner]
    strong = (owner == chosen) | (owner == (partner + parts // 2) % parts)
    return jnp.where(strong, factor * values, values)


def shard_levels(stream_key, extent, split, low, high):
    def one(dim, shards_of):
        heights = jax.random.uniform(jax.random.fold_in(jax.random.fold_in(stream_key, 6), dim), (shards_of,), jnp.float32, low / len(split), high / len(split))
        return jnp.repeat(jnp.exp(heights), extent[dim] // shards_of).reshape((-1,) + (1,) * (len(extent) - dim - 1))

    level = one(*split[0])
    for cut in split[1:]:
        level = level * one(*cut)
    return level


def noise(own_key, dims, scale, bound, cuts=(), kind=jnp.bfloat16):
    drawn = jax.random.normal(own_key, dims, jnp.float32) * scale
    if len(cuts) > 0:
        drawn = shard_levels(own_key, dims, cuts, -0.22, 0.18) * drawn
    return jnp.clip(drawn, min=-bound, max=bound).astype(kind)


def noise_with(stream_key, extent, scale, bound, shards, heavy, dtype=jnp.bfloat16):
    values = scale * jax.random.normal(stream_key, extent, jnp.float32)
    if shards:
        values = values * shard_levels(stream_key, extent, shards, -0.22, 0.18)
    return jnp.clip(spiked(values, jax.random.fold_in(stream_key, 3), *heavy), -bound, bound).astype(dtype)


def setup_inputs(seed: int = 0) -> dict:
    key_of = jax.random.split(jax.random.key(seed), 13)
    hidden_in = noise(key_of[0], (TOKENS, D), 1.0, 6.0, ((0, 32),), jnp.float32)
    qkv_weight = noise(key_of[1], (LAYERS, 2, D, 3, D), D ** -0.5, 0.21875, ((2, 16), (4, 2)))
    out_weight = noise(key_of[2], (LAYERS, 2, D, D), (D // 8) ** -0.5, 0.625, ((2, 2), (3, 16)))
    up_weight = noise(key_of[3], (LAYERS, D, FF), D ** -0.5, 0.21875, ((1, 16), (2, 2)))
    down_weight = noise(key_of[4], (LAYERS, FF, D), FF ** -0.5, 0.109375, ((1, 2), (2, 16)))
    qv_bias = noise(key_of[5], (LAYERS, 2, 2, D), 0.5, 3.0, ((3, 2),), jnp.float32)
    out_bias = noise(key_of[6], (LAYERS, 2, D), 0.5, 3.0, (), jnp.float32)
    up_bias = noise(key_of[7], (LAYERS, FF), 0.5, 3.0, ((1, 2),), jnp.float32)
    down_bias = noise(key_of[8], (LAYERS, D), 0.5, 3.0, (), jnp.float32)
    norm_gain = jnp.clip(1.0 + 0.15 * jax.random.normal(key_of[9], (LAYERS, 3, D), jnp.float32), 0.25, 1.75)
    norm_shift = noise(key_of[10], (LAYERS, 3, D), 0.3, 2.0, (), jnp.float32)
    cotangent = noise_with(key_of[11], (TOKENS, D), 1.0, 6.0, ((0, 32),), (0, 1, 32, 2.75), jnp.float32)
    return {"hidden_in": hidden_in, "qkv_weight": qkv_weight, "out_weight": out_weight, "up_weight": up_weight, "down_weight": down_weight, "qv_bias": qv_bias, "out_bias": out_bias, "up_bias": up_bias, "down_bias": down_bias, "norm_gain": norm_gain, "norm_shift": norm_shift, "cotangent": cotangent}


@jax.custom_vjp
def low(v):
    return lax.optimization_barrier(v.astype(jnp.bfloat16)).astype(jnp.float32)

@jax.custom_vjp
def low_back(v):
    return v

def low_keep(v):
    return (low(v), None)

def low_pass(kept, grad):
    return (grad,)

def back_keep(v):
    return (v, None)

def back_low(kept, grad):
    return (low(grad),)
low.defvjp(low_keep, low_pass)
low_back.defvjp(back_keep, back_low)
layer_eps = 1e-06

def layer_norm(values, norm_gain, norm_shift):
    average = lax.optimization_barrier(jnp.mean(values, axis=-1, keepdims=True))
    centred = values - average
    spread_sq = lax.optimization_barrier(jnp.mean(centred * centred, axis=-1, keepdims=True))
    return centred * lax.rsqrt(spread_sq + layer_eps) * norm_gain + norm_shift

def dense_high(left, right):
    return jnp.dot(left, right, precision=lax.Precision.HIGHEST, preferred_element_type=jnp.float32)

def attention(normalised_input, query_key_value_weight, bias_qv, output_weight_matrix):
    model_width = normalised_input.shape[-1]
    head_dim = model_width // HEADS
    rounded_value = low(normalised_input)
    projected_output = jnp.einsum('acx,xyp->acyp', rounded_value, query_key_value_weight, precision=lax.Precision.HIGHEST)
    offsets = jnp.stack([bias_qv[0], jnp.zeros_like(bias_qv[0]), bias_qv[1]], axis=0)
    projected_output = projected_output + offsets
    shaped = projected_output.reshape(projected_output.shape[0], projected_output.shape[1], 3, HEADS, head_dim)
    queries = low_back(low(shaped[:, :, 0]))
    keys_all = low_back(low(shaped[:, :, 1]))
    values_all = low_back(low(shaped[:, :, 2]))
    score_scale = head_dim ** (-0.5)
    scores = low_back(jnp.einsum('slhe,smhe->shlm', queries, keys_all, precision=lax.Precision.HIGHEST) * score_scale)
    weights_low = low(jax.nn.softmax(scores, axis=-1))
    attention_mixed = jnp.einsum('shlm,smhe->slhe', weights_low, values_all, precision=lax.Precision.HIGHEST)
    attention_mixed = low_back(low(attention_mixed.reshape(attention_mixed.shape[0], attention_mixed.shape[1], model_width)))
    return low_back(jnp.einsum('xum,mo->xuo', attention_mixed, output_weight_matrix, precision=lax.Precision.HIGHEST))

def clip_layers(tokens, params):
    qkv_w, out_w, up_w, down_w, qv_b, out_b, up_b, down_b, gains, shifts = params
    model_width = tokens.shape[-1]
    hidden = tokens
    for layer_at in range(LAYERS):
        normalised_input = layer_norm(hidden, gains[layer_at, 0], shifts[layer_at, 0]).reshape(FRAMES, PATCHES, model_width)
        branch = attention(normalised_input, qkv_w[layer_at, 0], qv_b[layer_at, 0], out_w[layer_at, 0])
        hidden = hidden + branch.reshape(-1, model_width) + out_b[layer_at, 0]
        normalised_input = layer_norm(hidden, gains[layer_at, 1], shifts[layer_at, 1]).reshape(FRAMES, PATCHES, model_width)
        branch = attention(jnp.swapaxes(normalised_input, 0, 1), qkv_w[layer_at, 1], qv_b[layer_at, 1], out_w[layer_at, 1])
        hidden = hidden + jnp.swapaxes(branch, 0, 1).reshape(-1, model_width) + out_b[layer_at, 1]
        normalised_input = low(layer_norm(hidden, gains[layer_at, 2], shifts[layer_at, 2]))
        inner_pre = low_back(dense_high(normalised_input, up_w[layer_at]) + up_b[layer_at])
        activated = low(jax.nn.gelu(inner_pre, approximate=False))
        hidden = hidden + low_back(dense_high(activated, down_w[layer_at])) + down_b[layer_at]
    return hidden

def reference(hidden_in, qkv_weight, out_weight, up_weight, down_weight, qv_bias, out_bias, up_bias, down_bias, norm_gain, norm_shift, cotangent):
    params = (qkv_weight.astype(jnp.float32), out_weight.astype(jnp.float32), up_weight.astype(jnp.float32), down_weight.astype(jnp.float32), qv_bias.astype(jnp.float32), out_bias.astype(jnp.float32), up_bias.astype(jnp.float32), down_bias.astype(jnp.float32), norm_gain.astype(jnp.float32), norm_shift.astype(jnp.float32))
    model_width = hidden_in.shape[-1]
    clip_rows = hidden_in.astype(jnp.float32).reshape(CLIPS, FRAMES * PATCHES, model_width)

    def forward(inputs, weights):

        def one_clip(tokens):
            return jax.checkpoint(clip_layers)(tokens, weights)
        return lax.map(one_clip, inputs)
    outputs, pullback = jax.vjp(forward, clip_rows, params)
    grad_clips, grad_params = pullback(cotangent.astype(jnp.float32).reshape(clip_rows.shape))
    return (outputs.reshape(TOKENS, model_width), grad_clips.reshape(TOKENS, model_width), grad_params[0], grad_params[1], grad_params[2], grad_params[3], grad_params[4], grad_params[5], grad_params[6], grad_params[7], grad_params[8], grad_params[9])
```

```python
import jax
import jax.numpy as jnp
from jax import lax
from jax.sharding import PartitionSpec as P

D = 768
FF = 3072
HEADS = 12
FRAMES = 16
PATCHES = 196
ROWS_AXES = ("col", "dp", "row")
ALL_AXES = ("dp", "row", "col")
CLIP_AXES = ("row", "col")
HEAD = D // HEADS
SCALE = HEAD**-0.5

layer_eps = 1e-06


def layer_norm(values, norm_gain, norm_shift):
    average = jnp.mean(values, axis=-1, keepdims=True)
    centred = values - average
    spread_sq = jnp.mean(centred * centred, axis=-1, keepdims=True)
    return centred * lax.rsqrt(spread_sq + layer_eps) * norm_gain + norm_shift


def exact_gelu(values):
    return jax.nn.gelu(values, approximate=False)


def dot(left, right, dims):
    return jnp.einsum(dims, left, right, preferred_element_type=jnp.float32)


def clip_place():
    return lax.axis_index("row") * lax.axis_size("col") + lax.axis_index("col")


def clip_swap(value, apart):
    count = lax.axis_size("row") * lax.axis_size("col")
    return lax.ppermute(value, CLIP_AXES, [(at, at ^ apart) for at in range(count)])


def to_patches(rows, group):
    own_frames = FRAMES // group
    share = PATCHES // group
    place = clip_place() % group
    grid = rows.reshape(own_frames, PATCHES, rows.shape[-1])
    total = jnp.zeros((FRAMES, share, rows.shape[-1]), rows.dtype)
    for apart in range(group):
        other = place ^ apart
        piece = lax.dynamic_slice_in_dim(grid, other * share, share, 1)
        if apart:
            piece = clip_swap(piece, apart)
        total = lax.dynamic_update_slice_in_dim(total, piece, other * own_frames, 0)
    return jnp.swapaxes(total, 0, 1)


def to_frames(rows, group):
    own_frames = FRAMES // group
    share = PATCHES // group
    place = clip_place() % group
    grid = jnp.swapaxes(rows, 0, 1)
    total = jnp.zeros((own_frames, PATCHES, rows.shape[-1]), rows.dtype)
    for apart in range(group):
        other = place ^ apart
        piece = lax.dynamic_slice_in_dim(grid, other * own_frames, own_frames, 0)
        if apart:
            piece = clip_swap(piece, apart)
        total = lax.dynamic_update_slice_in_dim(total, piece, other * share, 1)
    return total.reshape(own_frames * PATCHES, rows.shape[-1])


def heads_of(flat):
    return flat.reshape(flat.shape[:-1] + (HEADS, HEAD))


def attend(qkv):
    q, k, v = heads_of(qkv[0]), heads_of(qkv[1]), heads_of(qkv[2])
    scores = dot(q, k, "slhe,smhe->shlm") * SCALE
    top = jnp.max(scores, axis=-1, keepdims=True)
    raised = jnp.exp(scores - top)
    weights = raised / jnp.sum(raised, axis=-1, keepdims=True)
    mixed = dot(weights.astype(jnp.bfloat16), v, "shlm,smhe->slhe").astype(jnp.bfloat16)
    return mixed.reshape(qkv.shape[1:]), weights


def attend_back(qkv, weights, grad_mixed):
    q, k, v = heads_of(qkv[0]), heads_of(qkv[1]), heads_of(qkv[2])
    dm = heads_of(grad_mixed)
    dp = dot(dm, v, "slhe,smhe->shlm")
    dv = dot(weights.astype(jnp.bfloat16), dm, "shlm,slhe->smhe")
    ds = (weights * (dp - jnp.sum(dp * weights, axis=-1, keepdims=True))).astype(jnp.bfloat16)
    dq = dot(ds, k, "shlm,smhe->slhe") * SCALE
    dk = dot(ds, q, "shlm,slhe->smhe") * SCALE
    return jnp.stack([dq, dk, dv]).astype(jnp.bfloat16).reshape(qkv.shape)


def project(rows, weight, bias_pair):
    out = dot(rows, weight, "nd,dte->tne")
    offsets = jnp.stack([bias_pair[0], jnp.zeros_like(bias_pair[0]), bias_pair[1]])
    return (out + offsets[:, None, :]).astype(jnp.bfloat16)


def norm_back(values, gain, shift, grad_normed, carry):
    _, pull = jax.vjp(layer_norm, values, gain, shift)
    grad_values, grad_gain, grad_shift = pull(grad_normed)
    return carry + grad_values, grad_gain, grad_shift


def pack_rows(qkv_weight, out_weight, up_weight, down_weight, at):
    rows = up_weight.shape[1]
    return jnp.concatenate(
        [
            jnp.moveaxis(qkv_weight[at], 1, 0).reshape(rows, -1),
            jnp.moveaxis(out_weight[at], 2, 0).reshape(rows, -1),
            up_weight[at],
            down_weight[at].T,
        ],
        axis=1,
    )


def unpack_full(full, cols):
    half, units = D // cols, FF // cols
    qkv = full[:, :, : 6 * half].reshape(cols, D, 2, 3, half)
    qkv = jnp.transpose(qkv, (2, 1, 3, 0, 4)).reshape(2, D, 3, D)
    out = full[:, :, 6 * half : 8 * half].reshape(cols, D, 2, half)
    out = jnp.transpose(out, (2, 0, 3, 1)).reshape(2, D, D)
    up = jnp.transpose(full[:, :, 8 * half : 8 * half + units], (1, 0, 2)).reshape(D, FF)
    down = jnp.transpose(full[:, :, 8 * half + units :], (0, 2, 1)).reshape(FF, D)
    return qkv, out, up, down


def pack_grads(qkv, out, up, down, cols):
    half, units = D // cols, FF // cols
    qkv = jnp.transpose(qkv.reshape(2, D, 3, cols, half), (3, 1, 0, 2, 4)).reshape(cols, D, 6 * half)
    out = jnp.transpose(out.reshape(2, cols, half, D), (1, 3, 0, 2)).reshape(cols, D, 2 * half)
    up = jnp.transpose(up.reshape(D, cols, units), (1, 0, 2))
    down = jnp.transpose(down.reshape(cols, units, D), (0, 2, 1))
    return jnp.concatenate([qkv, out, up, down], axis=2).astype(jnp.bfloat16)


def unpack_own(rows, half, units):
    count = rows.shape[0]
    qkv = jnp.moveaxis(rows[:, : 6 * half].reshape(count, 2, 3, half), 0, 1)
    out = jnp.moveaxis(rows[:, 6 * half : 8 * half].reshape(count, 2, half), 0, 2)
    up = rows[:, 8 * half : 8 * half + units]
    down = rows[:, 8 * half + units :].T
    return qkv, out, up, down


def layer_forward(hidden, weights, small, group):
    qkv_w, out_w, up_w, down_w = weights
    gains, shifts, bias_qv, bias_out, bias_up, bias_down = small
    own_frames = FRAMES // group
    x0 = layer_norm(hidden, gains[0], shifts[0]).astype(jnp.bfloat16)
    qkv0 = project(x0, qkv_w[0], bias_qv[0]).reshape(3, own_frames, PATCHES, D)
    mixed0, p0 = attend(qkv0)
    mixed0 = mixed0.reshape(-1, D)
    hidden1 = hidden + dot(mixed0, out_w[0], "nc,cd->nd") + bias_out[0]
    x1 = layer_norm(hidden1, gains[1], shifts[1]).astype(jnp.bfloat16)
    x1 = to_patches(x1, group)
    share = x1.shape[0]
    x1 = x1.reshape(-1, D)
    qkv1 = project(x1, qkv_w[1], bias_qv[1]).reshape(3, share, FRAMES, D)
    mixed1, p1 = attend(qkv1)
    mixed1 = to_frames(mixed1, group)
    hidden2 = hidden1 + dot(mixed1, out_w[1], "nc,cd->nd") + bias_out[1]
    x2 = layer_norm(hidden2, gains[2], shifts[2]).astype(jnp.bfloat16)
    inner = dot(x2, up_w, "nd,df->nf") + bias_up
    act = exact_gelu(inner).astype(jnp.bfloat16)
    hidden3 = hidden2 + dot(act, down_w, "nf,fd->nd") + bias_down
    return hidden3, (hidden, hidden1, hidden2, x0, qkv0, p0, mixed0, x1, qkv1, p1, mixed1, x2, inner, act)


def bias_sums(d):
    flat = d.reshape(3, -1, D).astype(jnp.float32)
    return jnp.stack([jnp.sum(flat[0], axis=0), jnp.sum(flat[2], axis=0)])


def layer_backward(record, grad, weights, small, group, cols):
    hidden, hidden1, hidden2, x0, qkv0, p0, mixed0, x1, qkv1, p1, mixed1, x2, inner, act = record
    qkv_w, out_w, up_w, down_w = weights
    gains, shifts, *_ = small
    down_bias = jnp.sum(grad, axis=0)
    gb = grad.astype(jnp.bfloat16)
    _, pull = jax.vjp(exact_gelu, inner)
    d_inner = pull(dot(gb, down_w, "nd,fd->nf"))[0].astype(jnp.bfloat16)
    down_g = dot(act, gb, "nf,nd->fd")
    up_bias = jnp.sum(d_inner.astype(jnp.float32), axis=0)
    up_g = dot(x2, d_inner, "nd,nf->df")
    grad, gain2, shift2 = norm_back(hidden2, gains[2], shifts[2], dot(d_inner, up_w, "nf,df->nd"), grad)

    out_bias1 = jnp.sum(grad, axis=0)
    gb = grad.astype(jnp.bfloat16)
    out_g1 = dot(mixed1, gb, "nc,nd->cd")
    dm = to_patches(dot(gb, out_w[1], "nd,cd->nc").astype(jnp.bfloat16), group)
    d1 = attend_back(qkv1, p1, dm).reshape(3, -1, D)
    qv1 = bias_sums(d1)
    qkv_g1 = dot(x1, d1, "nd,tne->dte")
    dx = dot(d1, qkv_w[1], "tne,dte->nd").astype(jnp.bfloat16)
    dx = to_frames(dx.reshape(-1, FRAMES, D), group).astype(jnp.float32)
    grad, gain1, shift1 = norm_back(hidden1, gains[1], shifts[1], dx, grad)

    out_bias0 = jnp.sum(grad, axis=0)
    gb = grad.astype(jnp.bfloat16)
    out_g0 = dot(mixed0, gb, "nc,nd->cd")
    dm = dot(gb, out_w[0], "nd,cd->nc").astype(jnp.bfloat16).reshape(qkv0.shape[1:])
    d0 = attend_back(qkv0, p0, dm).reshape(3, -1, D)
    qv0 = bias_sums(d0)
    qkv_g0 = dot(x0, d0, "nd,tne->dte")
    dx = dot(d0, qkv_w[0], "tne,dte->nd")
    grad, gain0, shift0 = norm_back(hidden, gains[0], shifts[0], dx, grad)
    packed = pack_grads(jnp.stack([qkv_g0, qkv_g1]), jnp.stack([out_g0, out_g1]), up_g, down_g, cols)
    small_g = (
        jnp.stack([gain0, gain1, gain2]),
        jnp.stack([shift0, shift1, shift2]),
        jnp.stack([qv0, qv1]),
        jnp.stack([out_bias0, out_bias1]),
        up_bias,
        down_bias,
    )
    return grad, packed, small_g


def shards(
    hidden_in,
    qkv_weight,
    out_weight,
    up_weight,
    down_weight,
    qv_bias,
    out_bias,
    up_bias,
    down_bias,
    norm_gain,
    norm_shift,
    cotangent,
):
    layers = qkv_weight.shape[0]
    cols = lax.axis_size("col")
    group = FRAMES * PATCHES // hidden_in.shape[0]
    half, units = D // cols, FF // cols
    qv_all = lax.all_gather(qv_bias, "col", axis=3, tiled=True)
    up_all = lax.all_gather(up_bias, "col", axis=1, tiled=True)
    hidden = hidden_in
    kept = []
    for at in range(layers):
        packed = pack_rows(qkv_weight, out_weight, up_weight, down_weight, at)
        full = lax.all_gather(packed, ROWS_AXES, axis=0, tiled=True).reshape(cols, D, -1)
        weights = unpack_full(full, cols)
        small = (norm_gain[at], norm_shift[at], qv_all[at], out_bias[at], up_all[at], down_bias[at])
        hidden, record = layer_forward(hidden, weights, small, group)
        kept.append((weights, small, record))
    grad = cotangent
    owned = [None] * layers
    smalls = [None] * layers
    for at in reversed(range(layers)):
        weights, small, record = kept[at]
        grad, packed, smalls[at] = layer_backward(record, grad, weights, small, group, cols)
        rows = lax.psum_scatter(
            packed.reshape(cols * D, -1), ROWS_AXES, scatter_dimension=0, tiled=True
        ).astype(jnp.float32)
        owned[at] = unpack_own(rows, half, units)
    grads = [jnp.stack([owned[at][i] for at in range(layers)]) for i in range(4)]
    terms = [jnp.stack([smalls[at][i] for at in range(layers)]) for i in range(6)]
    gain, shift, qv, outb, upb, downb = lax.psum(tuple(terms), ALL_AXES)
    col_at = lax.axis_index("col")
    qv = lax.dynamic_slice_in_dim(qv, col_at * half, half, 3)
    upb = lax.dynamic_slice_in_dim(upb, col_at * units, units, 1)
    return (hidden, grad, *grads, qv, outb, upb, downb, gain, shift)


def solution(mesh):
    return jax.shard_map(
        shards,
        mesh=mesh,
        in_specs=(
            P(("dp", "row", "col"), None),
            P(None, None, ("dp", "row"), None, "col"),
            P(None, None, "col", ("dp", "row")),
            P(None, ("dp", "row"), "col"),
            P(None, "col", ("dp", "row")),
            P(None, None, None, "col"),
            P(),
            P(None, "col"),
            P(),
            P(),
            P(),
            P(("dp", "row", "col"), None),
        ),
        out_specs=(
            P(("dp", "row", "col"), None),
            P(("dp", "row", "col"), None),
            P(None, None, ("dp", "row"), None, "col"),
            P(None, None, "col", ("dp", "row")),
            P(None, ("dp", "row"), "col"),
            P(None, "col", ("dp", "row")),
            P(None, None, None, "col"),
            P(),
            P(None, "col"),
            P(),
            P(),
            P(),
        ),
        check_vma=False,
    )
```

```python
import functools

import jax
import jax.numpy as jnp
from jax import lax
from jax.experimental import pallas as pl
from jax.experimental.pallas import tpu as pltpu
from jax.sharding import PartitionSpec as P

D = 768
FF = 3072
HEADS = 12
FRAMES = 16
PATCHES = 196
ROWS_AXES = ("col", "dp", "row")
ALL_AXES = ("dp", "row", "col")
CLIP_AXES = ("row", "col")
HEAD = D // HEADS
PAIR = 2 * HEAD
SCALE = HEAD**-0.5
LAYER_EPS = 1e-06
NEG = -1e30

TILE = 8
FRAME_PAD = -(-PATCHES // 16) * 16
KEY_PAD = -(-PATCHES // 128) * 128
CHUNK = 512

BF = jnp.bfloat16
F32 = jnp.float32
ANY = pl.BlockSpec(memory_space=pl.ANY)
SMEM = pl.BlockSpec(memory_space=pltpu.SMEM)


def dot_nn(left, right):
    return lax.dot_general(left, right, (((1,), (0,)), ((), ())), preferred_element_type=F32)


def dot_nt(left, right):
    return lax.dot_general(left, right, (((1,), (1,)), ((), ())), preferred_element_type=F32)


def dot_tn(left, right):
    return lax.dot_general(left, right, (((0,), (0,)), ((), ())), preferred_element_type=F32)


def whole(shape):
    return pl.BlockSpec(shape, lambda *_: (0,) * len(shape))


def shaped(shape, dtype):
    return jax.ShapeDtypeStruct(shape, dtype)


def normalise(values):
    average = jnp.mean(values, axis=-1, keepdims=True)
    centred = values - average
    spread = jnp.mean(centred * centred, axis=-1, keepdims=True)
    inverse = lax.rsqrt(spread + LAYER_EPS)
    return centred * inverse, inverse


def norm_rows(values, gain, shift):
    normed, _ = normalise(values)
    return normed * gain + shift


def norm_rows_back(values, gain, dx, carry):
    normed, inverse = normalise(values)
    e = dx * gain
    first = jnp.mean(e, axis=-1, keepdims=True)
    second = jnp.mean(e * normed, axis=-1, keepdims=True)
    grad = carry + (e - first - normed * second) * inverse
    return (
        grad,
        jnp.sum(dx * normed, axis=0, keepdims=True),
        jnp.sum(dx, axis=0, keepdims=True),
    )


def gelu_parts(u):
    size = jnp.abs(u) * (0.5**0.5)
    t = pl.reciprocal(1.0 + 0.3275911 * size, approx=False)
    poly = 1.421413741 + t * (-1.453152027 + t * 1.061405429)
    poly = t * (0.254829592 + t * (-0.284496736 + t * poly))
    bell = jnp.exp(-size * size)
    tail = 0.5 * poly * bell
    cdf = jnp.where(u >= 0, 1.0 - tail, tail)
    return u * cdf, cdf + u * bell * 0.3989422804014327


def halves(value):
    lane = lax.broadcasted_iota(jnp.int32, value.shape, 1)
    zero = jnp.zeros_like(value)
    return jnp.where(lane < HEAD, value, zero), jnp.where(lane < HEAD, zero, value)


def soft(scores, valid):
    scores = jnp.where(valid, scores, NEG)
    top = jnp.max(scores, axis=-1, keepdims=True)
    raised = jnp.exp((scores - top) * SCALE)
    return raised * (1.0 / jnp.sum(raised, axis=-1, keepdims=True))


def attend_pair(q, k, v, valid):
    total = 0.0
    for kh, vh in zip(halves(k), halves(v)):
        weights = soft(dot_nt(q, kh), valid)
        total = total + dot_nn(weights.astype(BF), vh)
    return total.astype(BF)


def attend_pair_back(q, k, v, dm, valid):
    dq = dk = dv = 0.0
    for qh, kh, vh, dmh in zip(halves(q), halves(k), halves(v), halves(dm)):
        weights = soft(dot_nt(q, kh), valid)
        dp = dot_nt(dm, vh)
        ds = (weights * (dp - jnp.sum(dp * weights, axis=-1, keepdims=True))).astype(BF)
        dv = dv + dot_tn(weights.astype(BF), dmh)
        dq = dq + dot_nn(ds, kh)
        dk = dk + dot_tn(ds, qh)
    return (dq * SCALE).astype(BF), (dk * SCALE).astype(BF), dv.astype(BF)


def frame_valid():
    return lax.broadcasted_iota(jnp.int32, (FRAME_PAD, KEY_PAD), 1) < PATCHES


def patch_valid(rows):
    key = lax.broadcasted_iota(jnp.int32, (rows, rows), 1)
    query = lax.broadcasted_iota(jnp.int32, (rows, rows), 0)
    return (key % TILE) == (query % TILE)


def key_rows(value):
    return jnp.concatenate([value, jnp.zeros((KEY_PAD - FRAME_PAD, value.shape[1]), value.dtype)], 0)


def weight_scratch(cols, width):
    return pltpu.VMEM((cols, D, width), BF)


def load_weights(sources, target, sem):
    return [pltpu.make_async_copy(sources[0], target, sem)]


def start_all(copies):
    for copy in copies:
        copy.start()


def wait_all(copies):
    for copy in copies:
        copy.wait()


class Sizes:
    def __init__(self, tokens, cols):
        self.members = FRAMES * PATCHES // tokens
        self.frames = FRAMES // self.members
        self.groups = -(-PATCHES // (self.members * TILE))
        self.share = self.groups * TILE
        self.span = self.members * self.share
        self.piece = self.frames * TILE
        self.group_rows = self.members * self.piece
        self.rows = self.frames * FRAME_PAD
        self.patch_rows = self.groups * self.group_rows
        self.cols = cols
        self.half = D // cols
        self.units = FF // cols


def send_pieces(z, place_ref, spread_ref, piece_refs):
    for apart in range(z.members):
        start = (place_ref[0] ^ apart) * z.share
        for g in range(z.groups):
            parts = [
                spread_ref[pl.ds(pl.multiple_of(f * z.span + start + g * TILE, TILE), TILE), :]
                for f in range(z.frames)
            ]
            piece_refs[apart][g] = jnp.concatenate(parts, 0).astype(BF)


def take_pieces(z, place_ref, spread_ref, apart, rows):
    start = (place_ref[0] ^ apart) * z.share
    for g in range(z.groups):
        for f in range(z.frames):
            at = g * z.piece + f * TILE
            spread_ref[pl.ds(pl.multiple_of(f * z.span + start + g * TILE, TILE), TILE), :] = rows[
                at : at + TILE
            ]


def gather_groups(z, piece_refs, rows_ref):
    for g in range(z.groups):
        for m in range(z.members):
            at = g * z.group_rows + m * z.piece
            rows_ref[at : at + z.piece, :] = piece_refs[m][g]


def call(body, name, grid, in_specs, out_specs, out_shape, scratch, args, flops):
    moved = sum(a.size * a.dtype.itemsize for a in args) + sum(
        s.size * s.dtype.itemsize for s in out_shape
    )
    return pl.pallas_call(
        body,
        name=name,
        grid=grid,
        in_specs=in_specs,
        out_specs=out_specs,
        out_shape=out_shape,
        scratch_shapes=scratch,
        compiler_params=pltpu.CompilerParams(
            vmem_limit_bytes=58 * 2**20, dimension_semantics=("arbitrary",) * len(grid)
        ),
        cost_estimate=pl.CostEstimate(flops=int(flops), bytes_accessed=int(moved), transcendentals=0),
    )(*args)


def spatial_forward(z, place, hidden, wq, wo, bias, out_bias, gains, shifts):
    wide = 3 * z.half

    def body(place_ref, h_ref, *refs):
        wq_refs, refs = refs[: len(wq)], refs[len(wq) :]
        wo_refs, refs = refs[: len(wo)], refs[len(wo) :]
        bias_ref, ob_ref, gain_ref, shift_ref, *refs = refs
        x_ref, qkv_ref, mixed_ref, h1_ref, *refs = refs
        piece_refs, refs = refs[: z.members], refs[z.members :]
        wq_s, wo_s, qkv_s, mixed_s, spread, sem = refs
        f = pl.program_id(0)

        @pl.when(f == 0)
        def _():
            first = load_weights(wq_refs, wq_s, sem.at[0])
            later = load_weights(wo_refs, wo_s, sem.at[1])
            start_all(first)
            start_all(later)
            for at in range(z.frames):
                x_ref[at] = norm_rows(h_ref[at], gain_ref[0:1], shift_ref[0:1]).astype(BF)
            spread[...] = jnp.zeros_like(spread)
            wait_all(first)
            x = x_ref[...].reshape(z.rows, D)
            for c in range(z.cols):
                out = dot_nn(x, wq_s[c]) + bias_ref[c]
                qkv_s[:, c * wide : (c + 1) * wide] = out.astype(BF)
            wait_all(later)

        valid = frame_valid()
        rows = pl.ds(pl.multiple_of(f * FRAME_PAD, 16), FRAME_PAD)
        qkv_ref[0] = qkv_s[rows, :]
        for c in range(z.cols):
            for pair in range(z.half // PAIR):
                q, k, v = [
                    qkv_s[rows, pl.ds(c * wide + t * z.half + pair * PAIR, PAIR)] for t in range(3)
                ]
                at = c * z.half + pair * PAIR
                mixed_s[rows, at : at + PAIR] = attend_pair(q, key_rows(k), key_rows(v), valid)

        @pl.when(f == z.frames - 1)
        def _():
            branch = ob_ref[0:1]
            for c in range(z.cols):
                branch = branch + dot_nt(mixed_s[:, c * z.half : (c + 1) * z.half], wo_s[c])
            mixed_ref[...] = mixed_s[...].reshape(mixed_ref.shape)
            for at in range(z.frames):
                h1 = h_ref[at] + branch[at * FRAME_PAD : (at + 1) * FRAME_PAD]
                h1_ref[at] = h1
                spread[at * z.span : at * z.span + FRAME_PAD, :] = norm_rows(
                    h1, gain_ref[1:2], shift_ref[1:2]
                )
            send_pieces(z, place_ref, spread, piece_refs)

    frame = (z.frames, FRAME_PAD, D)
    piece = (z.groups, z.piece, D)
    return call(
        body,
        "spatial_forward",
        (z.frames,),
        [SMEM, whole(frame)]
        + [ANY] * (len(wq) + len(wo))
        + [whole(bias.shape), whole(out_bias.shape), whole(gains.shape), whole(shifts.shape)],
        [
            whole(frame),
            pl.BlockSpec((1, FRAME_PAD, 3 * D), lambda f: (f, 0, 0)),
            whole(frame),
            whole(frame),
        ]
        + [whole(piece)] * z.members,
        [
            shaped(frame, BF),
            shaped((z.frames, FRAME_PAD, 3 * D), BF),
            shaped(frame, BF),
            shaped(frame, F32),
        ]
        + [shaped(piece, BF)] * z.members,
        [
            weight_scratch(z.cols, wide),
            weight_scratch(z.cols, z.half),
            pltpu.VMEM((z.rows, 3 * D), BF),
            pltpu.VMEM((z.rows, D), BF),
            pltpu.VMEM((z.frames * z.span, D), F32),
            pltpu.SemaphoreType.DMA((2,)),
        ],
        (place, hidden, *wq, *wo, bias, out_bias, gains, shifts),
        2 * z.rows * D * (4 * D + 2 * KEY_PAD),
    )


def temporal_forward(z, pieces, wq, bias):
    wide = 3 * z.half
    n = z.group_rows

    def body(*refs):
        in_refs, refs = refs[: z.members], refs[z.members :]
        wq_refs, refs = refs[: len(wq)], refs[len(wq) :]
        bias_ref, qkv_ref, *refs = refs
        out_refs, refs = refs[: z.members], refs[z.members :]
        wq_s, x_s, qkv_s, sem = refs
        g = pl.program_id(0)

        @pl.when(g == 0)
        def _():
            copies = load_weights(wq_refs, wq_s, sem.at[0])
            start_all(copies)
            gather_groups(z, in_refs, x_s)
            wait_all(copies)
            x = x_s[...]
            for c in range(z.cols):
                out = dot_nn(x, wq_s[c]) + bias_ref[c]
                qkv_s[:, c * wide : (c + 1) * wide] = out.astype(BF)

        valid = patch_valid(n)
        rows = pl.ds(pl.multiple_of(g * n, n), n)
        qkv_ref[0] = qkv_s[rows, :]
        for c in range(z.cols):
            for pair in range(z.half // PAIR):
                q, k, v = [
                    qkv_s[rows, pl.ds(c * wide + t * z.half + pair * PAIR, PAIR)] for t in range(3)
                ]
                out = attend_pair(q, k, v, valid)
                at = c * z.half + pair * PAIR
                for m in range(z.members):
                    out_refs[m][0, :, at : at + PAIR] = out[m * z.piece : (m + 1) * z.piece]

    piece = (z.groups, z.piece, D)
    step = pl.BlockSpec((1, z.piece, D), lambda g: (g, 0, 0))
    return call(
        body,
        "temporal_forward",
        (z.groups,),
        [whole(piece)] * z.members + [ANY] * len(wq) + [whole(bias.shape)],
        [pl.BlockSpec((1, n, 3 * D), lambda g: (g, 0, 0))] + [step] * z.members,
        [shaped((z.groups, n, 3 * D), BF)] + [shaped(piece, BF)] * z.members,
        [
            weight_scratch(z.cols, wide),
            pltpu.VMEM((z.patch_rows, D), BF),
            pltpu.VMEM((z.patch_rows, 3 * D), BF),
            pltpu.SemaphoreType.DMA((1,)),
        ],
        (*pieces, *wq, bias),
        2 * z.patch_rows * D * (3 * D + 2 * n),
    )


def hidden_forward(z, place, pieces, hidden, wo, wu, wd, out_bias, up_bias, down_bias, gains, shifts):
    steps = FF // CHUNK
    per = z.units // CHUNK

    def body(place_ref, *refs):
        in_refs, refs = refs[: z.members], refs[z.members :]
        h1_ref, *refs = refs
        wo_refs, refs = refs[: len(wo)], refs[len(wo) :]
        wu_refs, refs = refs[: len(wu)], refs[len(wu) :]
        wd_refs, refs = refs[: len(wd)], refs[len(wd) :]
        ob_ref, ub_ref, db_ref, gain_ref, shift_ref, *refs = refs
        h2_ref, x_ref, act_ref, slope_ref, h3_ref, *refs = refs
        wo_s, wu_s, wd_s, spread, sem = refs
        i = pl.program_id(0)

        @pl.when(i == 0)
        def _():
            first = load_weights(wo_refs, wo_s, sem.at[0])
            second = load_weights(wu_refs, wu_s, sem.at[1])
            third = load_weights(wd_refs, wd_s, sem.at[2])
            start_all(first)
            start_all(second)
            start_all(third)
            wait_all(first)
            for m in range(z.members):
                mixed = in_refs[m][...].reshape(z.groups * z.piece, D)
                branch = 0.0
                for c in range(z.cols):
                    branch = branch + dot_nt(mixed[:, c * z.half : (c + 1) * z.half], wo_s[c])
                take_pieces(z, place_ref, spread, m, branch)
            for f in range(z.frames):
                rows = slice(f * FRAME_PAD, (f + 1) * FRAME_PAD)
                h2 = h1_ref[f] + spread[f * z.span : f * z.span + FRAME_PAD, :] + ob_ref[1:2]
                h2_ref[f] = h2
                x_ref[rows, :] = norm_rows(h2, gain_ref[2:3], shift_ref[2:3]).astype(BF)
                h3_ref[f] = h2 + db_ref[...]
            wait_all(second)
            wait_all(third)

        c = i // per
        cut = pl.ds(pl.multiple_of((i % per) * CHUNK, CHUNK), CHUNK)
        up = wu_s[c, :, cut]
        down = wd_s[c, :, cut]
        bias = ub_ref[...]
        for f in range(z.frames):
            rows = slice(f * FRAME_PAD, (f + 1) * FRAME_PAD)
            act, slope = gelu_parts(dot_nn(x_ref[rows, :], up) + bias)
            act = act.astype(BF)
            act_ref[rows, :] = act
            slope_ref[rows, :] = slope.astype(slope_ref.dtype)
            h3_ref[f] += dot_nt(act, down)

    frame = (z.frames, FRAME_PAD, D)
    piece = (z.groups, z.piece, D)
    step = pl.BlockSpec((z.rows, CHUNK), lambda i: (0, i))
    return call(
        body,
        "hidden_forward",
        (steps,),
        [SMEM]
        + [whole(piece)] * z.members
        + [whole(frame)]
        + [ANY] * (len(wo) + len(wu) + len(wd))
        + [
            whole(out_bias.shape),
            pl.BlockSpec((1, CHUNK), lambda i: (0, i)),
            whole(down_bias.shape),
            whole(gains.shape),
            whole(shifts.shape),
        ],
        [whole(frame), whole((z.rows, D)), step, step, whole(frame)],
        [
            shaped(frame, F32),
            shaped((z.rows, D), BF),
            shaped((z.rows, FF), BF),
            shaped((z.rows, FF), F32),
            shaped(frame, F32),
        ],
        [
            weight_scratch(z.cols, z.half),
            weight_scratch(z.cols, z.units),
            weight_scratch(z.cols, z.units),
            pltpu.VMEM((z.frames * z.span, D), F32),
            pltpu.SemaphoreType.DMA((3,)),
        ],
        (place, *pieces, hidden, *wo, *wu, *wd, out_bias, up_bias, down_bias, gains, shifts),
        2 * z.rows * D * (D + 2 * FF),
    )


def hidden_backward(z, place, grad, h2, slope, wu, wd, gains):
    steps = FF // CHUNK
    per = z.units // CHUNK

    def body(place_ref, g_ref, h2_ref, slope_ref, *refs):
        wu_refs, refs = refs[: len(wu)], refs[len(wu) :]
        wd_refs, refs = refs[: len(wd)], refs[len(wd) :]
        gain_ref, di_ref, gb_ref, g2_ref, sums_ref, *refs = refs
        piece_refs, refs = refs[: z.members], refs[z.members :]
        wu_s, wd_s, dx_s, spread, sem = refs
        i = pl.program_id(0)

        @pl.when(i == 0)
        def _():
            first = load_weights(wd_refs, wd_s, sem.at[0])
            second = load_weights(wu_refs, wu_s, sem.at[1])
            start_all(first)
            start_all(second)
            total = 0.0
            for f in range(z.frames):
                rows = slice(f * FRAME_PAD, (f + 1) * FRAME_PAD)
                g = g_ref[f]
                gb_ref[rows, :] = g.astype(BF)
                total = total + jnp.sum(g, axis=0, keepdims=True)
            sums_ref[0:1] = total
            dx_s[...] = jnp.zeros_like(dx_s)
            spread[...] = jnp.zeros_like(spread)
            wait_all(first)
            wait_all(second)

        c = i // per
        cut = pl.ds(pl.multiple_of((i % per) * CHUNK, CHUNK), CHUNK)
        up = wu_s[c, :, cut]
        down = wd_s[c, :, cut]
        for f in range(z.frames):
            rows = slice(f * FRAME_PAD, (f + 1) * FRAME_PAD)
            di = (dot_nn(gb_ref[rows, :], down) * slope_ref[rows, :]).astype(BF)
            di_ref[rows, :] = di
            dx_s[rows, :] += dot_nt(di, up)

        @pl.when(i == steps - 1)
        def _():
            out_b = gain_g = shift_g = 0.0
            for f in range(z.frames):
                rows = slice(f * FRAME_PAD, (f + 1) * FRAME_PAD)
                g2, gg, sg = norm_rows_back(h2_ref[f], gain_ref[2:3], dx_s[rows, :], g_ref[f])
                g2_ref[f] = g2
                spread[f * z.span : f * z.span + FRAME_PAD, :] = g2
                gain_g, shift_g = gain_g + gg, shift_g + sg
                out_b = out_b + jnp.sum(g2, axis=0, keepdims=True)
            sums_ref[1:2] = gain_g
            sums_ref[2:3] = shift_g
            sums_ref[3:4] = out_b
            send_pieces(z, place_ref, spread, piece_refs)

    frame = (z.frames, FRAME_PAD, D)
    piece = (z.groups, z.piece, D)
    step = pl.BlockSpec((z.rows, CHUNK), lambda i: (0, i))
    return call(
        body,
        "hidden_backward",
        (steps,),
        [SMEM, whole(frame), whole(frame), step]
        + [ANY] * (len(wu) + len(wd))
        + [whole(gains.shape)],
        [step, whole((z.rows, D)), whole(frame), whole((4, D))] + [whole(piece)] * z.members,
        [
            shaped((z.rows, FF), BF),
            shaped((z.rows, D), BF),
            shaped(frame, F32),
            shaped((4, D), F32),
        ]
        + [shaped(piece, BF)] * z.members,
        [
            weight_scratch(z.cols, z.units),
            weight_scratch(z.cols, z.units),
            pltpu.VMEM((z.rows, D), F32),
            pltpu.VMEM((z.frames * z.span, D), F32),
            pltpu.SemaphoreType.DMA((2,)),
        ],
        (place, grad, h2, slope, *wu, *wd, gains),
        2 * z.rows * D * 2 * FF,
    )


def temporal_backward(z, grad_pieces, qkv, wq, wo):
    wide = 3 * z.half
    n = z.group_rows

    def body(*refs):
        in_refs, refs = refs[: z.members], refs[z.members :]
        qkv_ref, *refs = refs
        wq_refs, refs = refs[: len(wq)], refs[len(wq) :]
        wo_refs, refs = refs[: len(wo)], refs[len(wo) :]
        d_ref, *refs = refs
        out_refs, refs = refs[: z.members], refs[z.members :]
        wq_s, wo_s, gb_s, dm_s, d_s, sem = refs
        g = pl.program_id(0)

        @pl.when(g == 0)
        def _():
            first = load_weights(wo_refs, wo_s, sem.at[0])
            start_all(first)
            start_all(load_weights(wq_refs, wq_s, sem.at[1]))
            gather_groups(z, in_refs, gb_s)
            wait_all(first)
            gb = gb_s[...]
            for c in range(z.cols):
                dm_s[:, c * z.half : (c + 1) * z.half] = dot_nn(gb, wo_s[c]).astype(BF)

        valid = patch_valid(n)
        rows = pl.ds(pl.multiple_of(g * n, n), n)
        for c in range(z.cols):
            for pair in range(z.half // PAIR):
                at = c * z.half + pair * PAIR
                q, k, v = [
                    qkv_ref[0, :, pl.ds(c * wide + t * z.half + pair * PAIR, PAIR)] for t in range(3)
                ]
                grads = attend_pair_back(q, k, v, dm_s[rows, at : at + PAIR], valid)
                for t in range(3):
                    col = c * wide + t * z.half + pair * PAIR
                    d_s[rows, col : col + PAIR] = grads[t]
        d_ref[...] = d_s[rows, :]

        @pl.when(g == z.groups - 1)
        def _():
            wait_all(load_weights(wq_refs, wq_s, sem.at[1]))
            dx = 0.0
            for c in range(z.cols):
                dx = dx + dot_nt(d_s[:, c * wide : (c + 1) * wide], wq_s[c])
            dx = dx.astype(BF)
            for gg in range(z.groups):
                for m in range(z.members):
                    at = gg * n + m * z.piece
                    out_refs[m][gg] = dx[at : at + z.piece]

    piece = (z.groups, z.piece, D)
    return call(
        body,
        "temporal_backward",
        (z.groups,),
        [whole(piece)] * z.members
        + [pl.BlockSpec((1, n, 3 * D), lambda g: (g, 0, 0))]
        + [ANY] * (len(wq) + len(wo)),
        [pl.BlockSpec((n, 3 * D), lambda g: (g, 0))] + [whole(piece)] * z.members,
        [shaped((z.patch_rows, 3 * D), BF)] + [shaped(piece, BF)] * z.members,
        [
            weight_scratch(z.cols, wide),
            weight_scratch(z.cols, z.half),
            pltpu.VMEM((z.patch_rows, D), BF),
            pltpu.VMEM((z.patch_rows, D), BF),
            pltpu.VMEM((z.patch_rows, 3 * D), BF),
            pltpu.SemaphoreType.DMA((2,)),
        ],
        (*grad_pieces, qkv, *wq, *wo),
        2 * z.patch_rows * D * (4 * D + 5 * n),
    )


def spatial_backward(z, place, dx_pieces, grad, h1, qkv, wo, gains):
    wide = 3 * z.half

    def body(place_ref, *refs):
        in_refs, refs = refs[: z.members], refs[z.members :]
        g_ref, h1_ref, qkv_ref, *refs = refs
        wo_refs, refs = refs[: len(wo)], refs[len(wo) :]
        gain_ref, gb_ref, d_ref, g1_ref, sums_ref, *refs = refs
        wo_s, spread, dm_s, sem = refs
        f = pl.program_id(0)

        @pl.when(f == 0)
        def _():
            first = load_weights(wo_refs, wo_s, sem.at[0])
            start_all(first)
            for m in range(z.members):
                rows = in_refs[m][...].reshape(z.groups * z.piece, D).astype(F32)
                take_pieces(z, place_ref, spread, m, rows)
            out_b = gain_g = shift_g = 0.0
            for at in range(z.frames):
                rows = slice(at * FRAME_PAD, (at + 1) * FRAME_PAD)
                dx = spread[at * z.span : at * z.span + FRAME_PAD, :]
                g1, gg, sg = norm_rows_back(h1_ref[at], gain_ref[1:2], dx, g_ref[at])
                g1_ref[at] = g1
                gb_ref[rows, :] = g1.astype(BF)
                gain_g, shift_g = gain_g + gg, shift_g + sg
                out_b = out_b + jnp.sum(g1, axis=0, keepdims=True)
            sums_ref[0:1] = gain_g
            sums_ref[1:2] = shift_g
            sums_ref[2:3] = out_b
            wait_all(first)
            gb = gb_ref[...]
            for c in range(z.cols):
                dm_s[:, c * z.half : (c + 1) * z.half] = dot_nn(gb, wo_s[c]).astype(BF)

        valid = frame_valid()
        rows = pl.ds(pl.multiple_of(f * FRAME_PAD, 16), FRAME_PAD)
        for c in range(z.cols):
            for pair in range(z.half // PAIR):
                at = c * z.half + pair * PAIR
                q, k, v = [
                    qkv_ref[0, :, pl.ds(c * wide + t * z.half + pair * PAIR, PAIR)] for t in range(3)
                ]
                dq, dk, dv = attend_pair_back(
                    q, key_rows(k), key_rows(v), dm_s[rows, at : at + PAIR], valid
                )
                for t, value in enumerate((dq, dk[:FRAME_PAD], dv[:FRAME_PAD])):
                    col = c * wide + t * z.half + pair * PAIR
                    d_ref[:, col : col + PAIR] = value

    frame = (z.frames, FRAME_PAD, D)
    piece = (z.groups, z.piece, D)
    return call(
        body,
        "spatial_backward",
        (z.frames,),
        [SMEM]
        + [whole(piece)] * z.members
        + [whole(frame), whole(frame), pl.BlockSpec((1, FRAME_PAD, 3 * D), lambda f: (f, 0, 0))]
        + [ANY] * len(wo)
        + [whole(gains.shape)],
        [
            whole((z.rows, D)),
            pl.BlockSpec((FRAME_PAD, 3 * D), lambda f: (f, 0)),
            whole(frame),
            whole((3, D)),
        ],
        [
            shaped((z.rows, D), BF),
            shaped((z.rows, 3 * D), BF),
            shaped(frame, F32),
            shaped((3, D), F32),
        ],
        [
            weight_scratch(z.cols, z.half),
            pltpu.VMEM((z.frames * z.span, D), F32),
            pltpu.VMEM((z.rows, D), BF),
            pltpu.SemaphoreType.DMA((1,)),
        ],
        (place, *dx_pieces, grad, h1, qkv, *wo, gains),
        2 * z.rows * D * (D + 5 * KEY_PAD),
    )


def input_backward(z, d, grad, hidden, wq, gains):
    wide = 3 * z.half

    def body(d_ref, g_ref, h_ref, *refs):
        wq_refs, refs = refs[: len(wq)], refs[len(wq) :]
        gain_ref, g0_ref, sums_ref, wq_s, sem = refs
        f = pl.program_id(0)

        @pl.when(f == 0)
        def _():
            copies = load_weights(wq_refs, wq_s, sem.at[0])
            start_all(copies)
            wait_all(copies)
            sums_ref[...] = jnp.zeros_like(sums_ref)

        dx = 0.0
        for c in range(z.cols):
            dx = dx + dot_nt(d_ref[:, c * wide : (c + 1) * wide], wq_s[c])
        for at in range(2):
            rows = slice(at * FRAME_PAD, (at + 1) * FRAME_PAD)
            g0, gg, sg = norm_rows_back(h_ref[at], gain_ref[0:1], dx[rows], g_ref[at])
            g0_ref[at] = g0
            sums_ref[0:1] += gg
            sums_ref[1:2] += sg

    frame = (z.frames, FRAME_PAD, D)
    step = pl.BlockSpec((2, FRAME_PAD, D), lambda f: (f, 0, 0))
    return call(
        body,
        "input_backward",
        (z.frames // 2,),
        [pl.BlockSpec((2 * FRAME_PAD, 3 * D), lambda f: (f, 0)), step, step]
        + [ANY] * len(wq)
        + [whole(gains.shape)],
        [step, whole((2, D))],
        [shaped(frame, F32), shaped((2, D), F32)],
        [weight_scratch(z.cols, wide), pltpu.SemaphoreType.DMA((1,))],
        (d, grad, hidden, *wq, gains),
        2 * z.rows * D * 3 * D,
    )


def weight_grad(z, name, left, right, step):
    total = right[0].shape[-1]
    width = total // z.cols
    per = width // step
    rows = sum(a.shape[0] for a in left)

    def body(*refs):
        left_refs, refs = refs[: len(left)], refs[len(left) :]
        right_refs, refs = refs[: len(right)], refs[len(right) :]
        out_ref, sums_ref, turned = refs

        @pl.when(pl.program_id(0) == 0)
        def _():
            parts = [r[...] for r in left_refs]
            value = parts[0] if len(parts) == 1 else jnp.concatenate(parts, 0)
            turned[...] = value.T

        parts = [r[...] for r in right_refs]
        value = parts[0] if len(parts) == 1 else jnp.concatenate(parts, 0)
        sums_ref[...] = jnp.sum(value.astype(F32), axis=0, keepdims=True)
        out_ref[0] = dot_nn(turned[...], value).astype(BF)

    return call(
        body,
        name,
        (total // step,),
        [whole(a.shape) for a in left]
        + [pl.BlockSpec((a.shape[0], step), lambda i: (0, i)) for a in right],
        [
            pl.BlockSpec((1, D, step), lambda i: (i // per, 0, i % per)),
            pl.BlockSpec((1, step), lambda i: (0, i)),
        ],
        [shaped((z.cols, D, width), BF), shaped((1, total), F32)],
        [pltpu.VMEM((D, rows), BF)],
        (*left, *right),
        2 * rows * D * total,
    )


def clip_swap(value, apart):
    count = lax.axis_size("row") * lax.axis_size("col")
    return lax.ppermute(value, CLIP_AXES, [(at, at ^ apart) for at in range(count)])


def swap_pieces(pieces):
    return [pieces[0]] + [clip_swap(pieces[apart], apart) for apart in range(1, len(pieces))]


def flat(pieces):
    return [p.reshape(-1, D) for p in pieces]


def pad_frames(z, rows):
    grid = rows.reshape(z.frames, PATCHES, D)
    return jnp.pad(grid, ((0, 0), (0, FRAME_PAD - PATCHES), (0, 0)))


def cut_frames(z, grid):
    return grid[:, :PATCHES].reshape(z.frames * PATCHES, D)


def layer_forward(z, place, hidden, w, small):
    gains, shifts, bias_qkv, bias_out, bias_up, bias_down = small
    x0, qkv0, mixed0, h1, *send = spatial_forward(
        z, place, hidden, w["qkv0"], w["out0"], bias_qkv[0], bias_out, gains, shifts
    )
    pieces = swap_pieces(send)
    qkv1, *back = temporal_forward(z, pieces, w["qkv1"], bias_qkv[1])
    mixed1 = swap_pieces(back)
    h2, x2, act, slope, h3 = hidden_forward(
        z, place, mixed1, h1, w["out1"], w["up"], w["down"], bias_out, bias_up, bias_down, gains, shifts
    )
    return h3, (hidden, x0, qkv0, mixed0, h1, pieces, qkv1, mixed1, h2, x2, act, slope)


def group_rows(z, pieces):
    stacked = jnp.stack(pieces, axis=1)
    return stacked.reshape(z.patch_rows, D)


def layer_backward(z, place, grad, record, w, small, spend):
    gains, *_ = small
    hidden, x0, qkv0, mixed0, h1, pieces, qkv1, mixed1, h2, x2, act, slope = record
    di, gb, g2, sums_h, *send = hidden_backward(z, place, grad, h2, slope, w["up"], w["down"], gains)
    got = swap_pieces(send)
    down_g, _ = weight_grad(z, "down_grad", [gb], [act], CHUNK)
    spend("down", down_g)
    up_g, up_b = weight_grad(z, "up_grad", [x2], [di], CHUNK)
    spend("up", up_g)
    out1_g, _ = weight_grad(z, "out1_grad", flat(send), flat(mixed1), z.half)
    spend("out1", out1_g)
    d1, *back = temporal_backward(z, got, qkv1, w["qkv1"], w["out1"])
    dx = swap_pieces(back)
    qkv1_g, qkv1_b = weight_grad(z, "qkv1_grad", [group_rows(z, pieces)], [d1], z.half)
    spend("qkv1", qkv1_g)
    gb, d0, g1, sums_s = spatial_backward(z, place, dx, g2, h1, qkv0, w["out0"], gains)
    out0_g, _ = weight_grad(z, "out0_grad", [gb], [mixed0.reshape(z.rows, D)], z.half)
    spend("out0", out0_g)
    qkv0_g, qkv0_b = weight_grad(z, "qkv0_grad", [x0.reshape(z.rows, D)], [d0], z.half)
    spend("qkv0", qkv0_g)
    g0, sums_i = input_backward(z, d0, g1, hidden, w["qkv0"], gains)

    def qv(sums):
        parts = sums.reshape(z.cols, 3, z.half)
        return jnp.stack([parts[:, 0].reshape(D), parts[:, 2].reshape(D)])

    small_g = (
        jnp.stack([sums_i[0], sums_s[0], sums_h[1]]),
        jnp.stack([sums_i[1], sums_s[1], sums_h[2]]),
        jnp.stack([qv(qkv0_b), qv(qkv1_b)]),
        jnp.stack([sums_s[2], sums_h[3]]),
        up_b[0],
        sums_h[0],
    )
    return g0, small_g


def own_parts(qkv_weight, out_weight, up_weight, down_weight, at):
    rows = up_weight.shape[1]
    return {
        "qkv0": qkv_weight[at, 0].reshape(rows, -1),
        "out0": out_weight[at, 0].T,
        "qkv1": qkv_weight[at, 1].reshape(rows, -1),
        "out1": out_weight[at, 1].T,
        "up": up_weight[at],
        "down": down_weight[at].T,
    }


PARTS = ("qkv0", "out0", "qkv1", "out1", "up", "down")


def fetch(parts, cols):
    packed = jnp.concatenate([parts[name] for name in PARTS], axis=1)
    full = lax.all_gather(packed, ROWS_AXES, axis=0, tiled=True).reshape(cols, D, -1)
    result, at = {}, 0
    for name in PARTS:
        width = parts[name].shape[1]
        result[name] = [full[:, :, at : at + width]]
        at += width
    return result


def scatter(grads, cols):
    packed = jnp.concatenate([grads[name] for name in PARTS], axis=2)
    own = lax.psum_scatter(packed.reshape(cols * D, -1), ROWS_AXES, scatter_dimension=0, tiled=True)
    result, at = {}, 0
    for name in PARTS:
        width = grads[name].shape[2]
        result[name] = own[:, at : at + width].astype(F32)
        at += width
    return result


def shards(
    hidden_in,
    qkv_weight,
    out_weight,
    up_weight,
    down_weight,
    qv_bias,
    out_bias,
    up_bias,
    down_bias,
    norm_gain,
    norm_shift,
    cotangent,
):
    layers = qkv_weight.shape[0]
    cols = lax.axis_size("col")
    z = Sizes(hidden_in.shape[0], cols)
    place = lax.axis_index("row") * cols + lax.axis_index("col")
    place = (place % z.members).astype(jnp.int32).reshape(1)
    qv_all = lax.all_gather(qv_bias, "col", axis=3)
    up_all = lax.all_gather(up_bias, "col", axis=1, tiled=True)
    zero = jnp.zeros_like(qv_all[:, :, 0])
    bias_qkv = jnp.stack([qv_all[:, :, 0], zero, qv_all[:, :, 1]], axis=3)
    bias_qkv = bias_qkv.reshape(layers, 2, cols, 1, 3 * z.half)
    hidden = pad_frames(z, hidden_in)
    kept = []
    for at in range(layers):
        w = fetch(own_parts(qkv_weight, out_weight, up_weight, down_weight, at), cols)
        small = (
            norm_gain[at],
            norm_shift[at],
            bias_qkv[at],
            out_bias[at],
            up_all[at][None],
            down_bias[at][None],
        )
        hidden, record = layer_forward(z, place, hidden, w, small)
        kept.append((w, small, record))
    grad = pad_frames(z, cotangent)
    owned = [None] * layers
    smalls = [None] * layers
    for at in reversed(range(layers)):
        w, small, record = kept[at]
        grads = {}
        grad, smalls[at] = layer_backward(z, place, grad, record, w, small, grads.__setitem__)
        owned[at] = scatter(grads, cols)
    rows = up_weight.shape[1]

    def both(make):
        return jnp.stack([make(owned[at]) for at in range(layers)])

    grad_qkv = both(
        lambda o: jnp.stack([o["qkv0"].reshape(rows, 3, -1), o["qkv1"].reshape(rows, 3, -1)])
    )
    grad_out = both(lambda o: jnp.stack([o["out0"].T, o["out1"].T]))
    grad_up = both(lambda o: o["up"])
    grad_down = both(lambda o: o["down"].T)
    terms = [jnp.stack([smalls[at][i] for at in range(layers)]) for i in range(6)]
    gain, shift, qv, outb, upb, downb = lax.psum(tuple(terms), ALL_AXES)
    col_at = lax.axis_index("col")
    qv = lax.dynamic_slice_in_dim(qv, col_at * z.half, z.half, 3)
    upb = lax.dynamic_slice_in_dim(upb, col_at * z.units, z.units, 1)
    return (
        cut_frames(z, hidden),
        cut_frames(z, grad),
        grad_qkv,
        grad_out,
        grad_up,
        grad_down,
        qv,
        outb,
        upb,
        downb,
        gain,
        shift,
    )


def solution(mesh):
    return jax.shard_map(
        shards,
        mesh=mesh,
        in_specs=(
            P(("dp", "row", "col"), None),
            P(None, None, ("dp", "row"), None, "col"),
            P(None, None, "col", ("dp", "row")),
            P(None, ("dp", "row"), "col"),
            P(None, "col", ("dp", "row")),
            P(None, None, None, "col"),
            P(),
            P(None, "col"),
            P(),
            P(),
            P(),
            P(("dp", "row", "col"), None),
        ),
        out_specs=(
            P(("dp", "row", "col"), None),
            P(("dp", "row", "col"), None),
            P(None, None, ("dp", "row"), None, "col"),
            P(None, None, "col", ("dp", "row")),
            P(None, ("dp", "row"), "col"),
            P(None, "col", ("dp", "row")),
            P(None, None, None, "col"),
            P(),
            P(None, "col"),
            P(),
            P(),
            P(),
        ),
        check_vma=False,
    )
```

```python
import math

import functools

import jax
import jax.numpy as jnp
from jax import lax
from jax.experimental import pallas as pl
from jax.experimental.pallas import tpu as pltpu
from jax.sharding import PartitionSpec as P

D = 768
FF = 3072
HEADS = 12
FRAMES = 16
PATCHES = 196
ROWS_AXES = ("col", "dp", "row")
ALL_AXES = ("dp", "row", "col")
CLIP_AXES = ("row", "col")
HEAD = D // HEADS
PAIR = 2 * HEAD
SCALE = HEAD**-0.5
LAYER_EPS = 1e-06
NEG = -1e30

TILE = 8
FRAME_PAD = -(-PATCHES // 16) * 16
KEY_PAD = -(-PATCHES // 128) * 128
CHUNK = 512

BF = jnp.bfloat16
F32 = jnp.float32
HBM = pl.BlockSpec(memory_space=pltpu.HBM)
SMEM = pl.BlockSpec(memory_space=pltpu.SMEM)


def dot_nn(left, right):
    return lax.dot_general(left, right, (((1,), (0,)), ((), ())), preferred_element_type=F32)


def dot_nt(left, right):
    return lax.dot_general(left, right, (((1,), (1,)), ((), ())), preferred_element_type=F32)


def dot_tn(left, right):
    return lax.dot_general(left, right, (((0,), (0,)), ((), ())), preferred_element_type=F32)


def whole(shape):
    return pl.BlockSpec(shape, lambda *_: (0,) * len(shape))


def shaped(shape, dtype):
    return jax.ShapeDtypeStruct(shape, dtype)


def normalise(values):
    average = jnp.mean(values, axis=-1, keepdims=True)
    centred = values - average
    spread = jnp.mean(centred * centred, axis=-1, keepdims=True)
    inverse = lax.rsqrt(spread + LAYER_EPS)
    return centred * inverse, inverse


def norm_rows(values, gain, shift):
    normed, _ = normalise(values)
    return normed * gain + shift


def norm_rows_back(values, gain, dx, carry):
    normed, inverse = normalise(values)
    e = dx * gain
    first = jnp.mean(e, axis=-1, keepdims=True)
    second = jnp.mean(e * normed, axis=-1, keepdims=True)
    grad = carry + (e - first - normed * second) * inverse
    return (
        grad,
        jnp.sum(dx * normed, axis=0, keepdims=True),
        jnp.sum(dx, axis=0, keepdims=True),
    )


def gelu_parts(u):
    size = jnp.abs(u) * (0.5**0.5)
    t = pl.reciprocal(1.0 + 0.3275911 * size, approx=False)
    poly = 1.421413741 + t * (-1.453152027 + t * 1.061405429)
    poly = t * (0.254829592 + t * (-0.284496736 + t * poly))
    bell = jnp.exp(-size * size)
    tail = 0.5 * poly * bell
    cdf = jnp.where(u >= 0, 1.0 - tail, tail)
    return u * cdf, cdf + u * bell * 0.3989422804014327


def halves(value):
    lane = lax.broadcasted_iota(jnp.int32, value.shape, 1)
    zero = jnp.zeros_like(value)
    return jnp.where(lane < HEAD, value, zero), jnp.where(lane < HEAD, zero, value)


def soft(scores, valid):
    scores = jnp.where(valid, scores, NEG)
    top = jnp.max(scores, axis=-1, keepdims=True)
    raised = jnp.exp((scores - top) * SCALE)
    return raised * (1.0 / jnp.sum(raised, axis=-1, keepdims=True))


def split_all(values):
    return [half for value in values for half in halves(value)]


def attend_all(q, k, v, valid):
    keys, values = split_all(k), split_all(v)
    scores = [dot_nt(q[h // 2], keys[h]) for h in range(len(keys))]
    weights = [soft(s, valid).astype(BF) for s in scores]
    mixed = [dot_nn(w, value) for w, value in zip(weights, values)]
    return [(mixed[h] + mixed[h + 1]).astype(BF) for h in range(0, len(mixed), 2)]


def attend_all_back(q, k, v, dm, valid):
    queries, keys, values, grads = split_all(q), split_all(k), split_all(v), split_all(dm)
    heads = range(len(keys))
    scores = [dot_nt(q[h // 2], keys[h]) for h in heads]
    dps = [dot_nt(dm[h // 2], values[h]) for h in heads]
    weights = [soft(s, valid) for s in scores]
    ds = [
        (w * (dp - jnp.sum(dp * w, axis=-1, keepdims=True))).astype(BF)
        for w, dp in zip(weights, dps)
    ]
    weights = [w.astype(BF) for w in weights]
    result = []
    for h in range(0, len(keys), 2):
        dv = dot_tn(weights[h], grads[h]) + dot_tn(weights[h + 1], grads[h + 1])
        dq = dot_nn(ds[h], keys[h]) + dot_nn(ds[h + 1], keys[h + 1])
        dk = dot_tn(ds[h], queries[h]) + dot_tn(ds[h + 1], queries[h + 1])
        result.append(((dq * SCALE).astype(BF), (dk * SCALE).astype(BF), dv.astype(BF)))
    return result


def pair_columns(z):
    for c in range(z.cols):
        for pair in range(z.half // PAIR):
            at = c * z.half + pair * PAIR
            starts = [(3 * c + t) * z.half + pair * PAIR for t in range(3)] + [at]
            yield [slice(start, start + PAIR) for start in starts]


def frame_valid():
    return lax.broadcasted_iota(jnp.int32, (FRAME_PAD, KEY_PAD), 1) < PATCHES


def patch_valid(rows):
    key = lax.broadcasted_iota(jnp.int32, (rows, rows), 1)
    query = lax.broadcasted_iota(jnp.int32, (rows, rows), 0)
    return (key % TILE) == (query % TILE)


def key_rows(value):
    return jnp.concatenate([value, jnp.zeros((KEY_PAD - FRAME_PAD, value.shape[1]), value.dtype)], 0)


class Weight:
    def __init__(self, packed, at, width):
        self.arrays = [packed]
        self.at = at
        self.width = width

    def scratch(self):
        return pltpu.VMEM((self.arrays[0].shape[0], D, self.width), BF)

    def step(self, size):
        per, first = self.width // size, self.at // size
        return pl.BlockSpec((1, D, size), lambda i: (i // per, 0, first + i % per))

    def copies(self, refs, target, sem):
        window = refs[0].at[:, :, pl.ds(self.at, self.width)]
        return [pltpu.make_async_copy(window, target, sem)]


def start_all(copies):
    for copy in copies:
        copy.start()


def wait_all(copies):
    for copy in copies:
        copy.wait()


class Sizes:
    def __init__(self, tokens, block, depth, row_count, cols):
        self.members = FRAMES * PATCHES // tokens
        self.frames = FRAMES // self.members
        self.groups = -(-PATCHES // (self.members * TILE))
        self.share = self.groups * TILE
        self.span = self.members * self.share
        self.piece = self.frames * TILE
        self.group_rows = self.members * self.piece
        self.rows = self.frames * FRAME_PAD
        self.patch_rows = self.groups * self.group_rows
        self.cols = cols
        self.half = D // cols
        self.units = FF // cols
        self.block = block
        self.depth = depth
        self.direct = block % 16 == 0 and cols == 2 and row_count == 2 and depth >= 2


def send_pieces(z, place_ref, spread_ref, piece_refs):
    for apart in range(z.members):
        start = (place_ref[0] ^ apart) * z.share
        for g in range(z.groups):
            parts = [
                spread_ref[pl.ds(pl.multiple_of(f * z.span + start + g * TILE, TILE), TILE), :]
                for f in range(z.frames)
            ]
            piece_refs[apart][g] = jnp.concatenate(parts, 0).astype(BF)


def take_pieces(z, place_ref, spread_ref, apart, rows):
    start = (place_ref[0] ^ apart) * z.share
    for g in range(z.groups):
        for f in range(z.frames):
            at = g * z.piece + f * TILE
            spread_ref[pl.ds(pl.multiple_of(f * z.span + start + g * TILE, TILE), TILE), :] = rows[
                at : at + TILE
            ]


def gather_groups(z, piece_refs, rows_ref):
    for g in range(z.groups):
        for m in range(z.members):
            at = g * z.group_rows + m * z.piece
            rows_ref[at : at + z.piece, :] = piece_refs[m][g]


def vmem_bytes(specs, arrays, scratch):
    total = 16 * 2**20
    for spec, array in zip(specs, arrays):
        if spec.block_shape is not None:
            total += 2 * math.prod(spec.block_shape) * array.dtype.itemsize
    for held in scratch:
        if held.memory_space == pltpu.VMEM:
            total += math.prod(held.shape) * jnp.dtype(held.dtype).itemsize
    return min(total, 58 * 2**20)


def call(body, name, grid, in_specs, out_specs, out_shape, scratch, args, flops):
    limit = vmem_bytes([*in_specs, *out_specs], [*args, *out_shape], scratch)
    moved = sum(a.size * a.dtype.itemsize for a in args) + sum(
        s.size * s.dtype.itemsize for s in out_shape
    )
    return pl.pallas_call(
        body,
        name=name,
        grid=grid,
        in_specs=in_specs,
        out_specs=out_specs,
        out_shape=out_shape,
        scratch_shapes=scratch,
        compiler_params=pltpu.CompilerParams(
            vmem_limit_bytes=limit, dimension_semantics=("arbitrary",) * len(grid)
        ),
        cost_estimate=pl.CostEstimate(flops=int(flops), bytes_accessed=int(moved), transcendentals=0),
    )(*args)


def spatial_forward(z, place, hidden, wq, wo, bias, out_bias, gains, shifts):
    wide = 3 * z.half

    def body(place_ref, h_ref, *refs):
        wq_refs, refs = refs[: len(wq.arrays)], refs[len(wq.arrays) :]
        wo_refs, refs = refs[: len(wo.arrays)], refs[len(wo.arrays) :]
        bias_ref, ob_ref, gain_ref, shift_ref, *refs = refs
        x_ref, qkv_ref, mixed_ref, h1_ref, *refs = refs
        piece_refs, refs = refs[: z.members], refs[z.members :]
        wq_s, wo_s, qkv_s, mixed_s, spread, sem = refs
        f = pl.program_id(0)

        @pl.when(f == 0)
        def _():
            first = wq.copies(wq_refs, wq_s, sem.at[0])
            later = wo.copies(wo_refs, wo_s, sem.at[1])
            start_all(first)
            start_all(later)
            for at in range(z.frames):
                x_ref[at] = norm_rows(h_ref[at], gain_ref[0:1], shift_ref[0:1]).astype(BF)
            spread[...] = jnp.zeros_like(spread)
            wait_all(first)
            x = x_ref[...].reshape(z.rows, D)
            for c in range(z.cols):
                out = dot_nn(x, wq_s[c]) + bias_ref[c]
                qkv_s[:, c * wide : (c + 1) * wide] = out.astype(BF)
            wait_all(later)

        rows = pl.ds(pl.multiple_of(f * FRAME_PAD, 16), FRAME_PAD)
        q, k, v = [[qkv_s[rows, at[t]] for at in pair_columns(z)] for t in range(3)]
        mixed = attend_all(q, [key_rows(x) for x in k], [key_rows(x) for x in v], frame_valid())
        qkv_ref[0] = qkv_s[rows, :]
        for at, value in zip(pair_columns(z), mixed):
            mixed_s[rows, at[3]] = value

        @pl.when(f == z.frames - 1)
        def _():
            branch = ob_ref[0:1]
            for c in range(z.cols):
                branch = branch + dot_nt(mixed_s[:, c * z.half : (c + 1) * z.half], wo_s[c])
            mixed_ref[...] = mixed_s[...].reshape(mixed_ref.shape)
            for at in range(z.frames):
                h1 = h_ref[at] + branch[at * FRAME_PAD : (at + 1) * FRAME_PAD]
                h1_ref[at] = h1
                spread[at * z.span : at * z.span + FRAME_PAD, :] = norm_rows(
                    h1, gain_ref[1:2], shift_ref[1:2]
                )
            send_pieces(z, place_ref, spread, piece_refs)

    frame = (z.frames, FRAME_PAD, D)
    piece = (z.groups, z.piece, D)
    return call(
        body,
        "spatial_forward",
        (z.frames,),
        [SMEM, whole(frame)]
        + [HBM] * (len(wq.arrays) + len(wo.arrays))
        + [whole(bias.shape), whole(out_bias.shape), whole(gains.shape), whole(shifts.shape)],
        [
            whole(frame),
            pl.BlockSpec((1, FRAME_PAD, 3 * D), lambda f: (f, 0, 0)),
            whole(frame),
            whole(frame),
        ]
        + [whole(piece)] * z.members,
        [
            shaped(frame, BF),
            shaped((z.frames, FRAME_PAD, 3 * D), BF),
            shaped(frame, BF),
            shaped(frame, F32),
        ]
        + [shaped(piece, BF)] * z.members,
        [
            wq.scratch(),
            wo.scratch(),
            pltpu.VMEM((z.rows, 3 * D), BF),
            pltpu.VMEM((z.rows, D), BF),
            pltpu.VMEM((z.frames * z.span, D), F32),
            pltpu.SemaphoreType.DMA((2,)),
        ],
        (place, hidden, *wq.arrays, *wo.arrays, bias, out_bias, gains, shifts),
        2 * z.rows * D * (4 * D + 2 * KEY_PAD),
    )


def temporal_forward(z, pieces, wq, bias):
    wide = 3 * z.half
    n = z.group_rows

    def body(*refs):
        in_refs, refs = refs[: z.members], refs[z.members :]
        wq_refs, refs = refs[: len(wq.arrays)], refs[len(wq.arrays) :]
        bias_ref, qkv_ref, *refs = refs
        out_refs, refs = refs[: z.members], refs[z.members :]
        wq_s, x_s, qkv_s, sem = refs
        g = pl.program_id(0)

        @pl.when(g == 0)
        def _():
            copies = wq.copies(wq_refs, wq_s, sem.at[0])
            start_all(copies)
            gather_groups(z, in_refs, x_s)
            wait_all(copies)
            x = x_s[...]
            for c in range(z.cols):
                out = dot_nn(x, wq_s[c]) + bias_ref[c]
                qkv_s[:, c * wide : (c + 1) * wide] = out.astype(BF)

        rows = pl.ds(pl.multiple_of(g * n, n), n)
        q, k, v = [[qkv_s[rows, at[t]] for at in pair_columns(z)] for t in range(3)]
        mixed = attend_all(q, k, v, patch_valid(n))
        qkv_ref[0] = qkv_s[rows, :]
        for at, value in zip(pair_columns(z), mixed):
            for m in range(z.members):
                out_refs[m][0, :, at[3]] = value[m * z.piece : (m + 1) * z.piece]

    piece = (z.groups, z.piece, D)
    step = pl.BlockSpec((1, z.piece, D), lambda g: (g, 0, 0))
    return call(
        body,
        "temporal_forward",
        (z.groups,),
        [whole(piece)] * z.members + [HBM] * len(wq.arrays) + [whole(bias.shape)],
        [pl.BlockSpec((1, n, 3 * D), lambda g: (g, 0, 0))] + [step] * z.members,
        [shaped((z.groups, n, 3 * D), BF)] + [shaped(piece, BF)] * z.members,
        [
            wq.scratch(),
            pltpu.VMEM((z.patch_rows, D), BF),
            pltpu.VMEM((z.patch_rows, 3 * D), BF),
            pltpu.SemaphoreType.DMA((1,)),
        ],
        (*pieces, *wq.arrays, bias),
        2 * z.patch_rows * D * (3 * D + 2 * n),
    )


def hidden_forward(z, place, pieces, hidden, wo, wu, wd, out_bias, up_bias, down_bias, gains, shifts):
    steps = FF // CHUNK

    def body(place_ref, *refs):
        in_refs, refs = refs[: z.members], refs[z.members :]
        h1_ref, *refs = refs
        wo_refs, refs = refs[: len(wo.arrays)], refs[len(wo.arrays) :]
        up_ref, down_ref, ob_ref, ub_ref, db_ref, gain_ref, shift_ref, *refs = refs
        h2_ref, x_ref, act_ref, slope_ref, h3_ref, *refs = refs
        wo_s, spread, sem = refs
        i = pl.program_id(0)

        @pl.when(i == 0)
        def _():
            first = wo.copies(wo_refs, wo_s, sem.at[0])
            start_all(first)
            wait_all(first)
            for m in range(z.members):
                mixed = in_refs[m][...].reshape(z.groups * z.piece, D)
                branch = 0.0
                for c in range(z.cols):
                    branch = branch + dot_nt(mixed[:, c * z.half : (c + 1) * z.half], wo_s[c])
                take_pieces(z, place_ref, spread, m, branch)
            for f in range(z.frames):
                rows = slice(f * FRAME_PAD, (f + 1) * FRAME_PAD)
                h2 = h1_ref[f] + spread[f * z.span : f * z.span + FRAME_PAD, :] + ob_ref[1:2]
                h2_ref[f] = h2
                x_ref[rows, :] = norm_rows(h2, gain_ref[2:3], shift_ref[2:3]).astype(BF)
                h3_ref[f] = h2 + db_ref[...]

        up, down, bias = up_ref[0], down_ref[0], ub_ref[...]
        blocks = [slice(f * FRAME_PAD, (f + 1) * FRAME_PAD) for f in range(z.frames)]
        inner = dot_nn(x_ref[blocks[0], :], up) + bias
        results = []
        for f in range(z.frames):
            later = dot_nn(x_ref[blocks[f + 1], :], up) + bias if f + 1 < z.frames else None
            act, slope = gelu_parts(inner)
            act = act.astype(BF)
            results.append((act, slope, dot_nt(act, down)))
            inner = later
        for f, (act, slope, out) in enumerate(results):
            act_ref[blocks[f], :] = act
            slope_ref[blocks[f], :] = slope
            h3_ref[f] += out

    frame = (z.frames, FRAME_PAD, D)
    piece = (z.groups, z.piece, D)
    step = pl.BlockSpec((z.rows, CHUNK), lambda i: (0, i))
    return call(
        body,
        "hidden_forward",
        (steps,),
        [SMEM]
        + [whole(piece)] * z.members
        + [whole(frame)]
        + [HBM] * len(wo.arrays)
        + [
            wu.step(CHUNK),
            wd.step(CHUNK),
            whole(out_bias.shape),
            pl.BlockSpec((1, CHUNK), lambda i: (0, i)),
            whole(down_bias.shape),
            whole(gains.shape),
            whole(shifts.shape),
        ],
        [whole(frame), whole((z.rows, D)), step, step, whole(frame)],
        [
            shaped(frame, F32),
            shaped((z.rows, D), BF),
            shaped((z.rows, FF), BF),
            shaped((z.rows, FF), F32),
            shaped(frame, F32),
        ],
        [
            wo.scratch(),
            pltpu.VMEM((z.frames * z.span, D), F32),
            pltpu.SemaphoreType.DMA((1,)),
        ],
        (place, *pieces, hidden, *wo.arrays, *wu.arrays, *wd.arrays, out_bias, up_bias, down_bias, gains, shifts),
        2 * z.rows * D * (D + 2 * FF),
    )


def hidden_backward(z, place, grad, h2, slope, wu, wd, gains):
    steps = FF // CHUNK

    def body(place_ref, g_ref, h2_ref, slope_ref, *refs):
        up_ref, down_ref, gain_ref, di_ref, gb_ref, g2_ref, sums_ref, *refs = refs
        piece_refs, refs = refs[: z.members], refs[z.members :]
        dx_s, spread = refs
        i = pl.program_id(0)

        @pl.when(i == 0)
        def _():
            total = 0.0
            for f in range(z.frames):
                rows = slice(f * FRAME_PAD, (f + 1) * FRAME_PAD)
                g = g_ref[f]
                gb_ref[rows, :] = g.astype(BF)
                total = total + jnp.sum(g, axis=0, keepdims=True)
            sums_ref[0:1] = total
            dx_s[...] = jnp.zeros_like(dx_s)
            spread[...] = jnp.zeros_like(spread)

        up, down = up_ref[0], down_ref[0]
        blocks = [slice(f * FRAME_PAD, (f + 1) * FRAME_PAD) for f in range(z.frames)]
        products = [dot_nn(gb_ref[rows, :], down) for rows in blocks]
        inner = [(p * slope_ref[rows, :]).astype(BF) for p, rows in zip(products, blocks)]
        outs = [dot_nt(di, up) for di in inner]
        for rows, di, out in zip(blocks, inner, outs):
            di_ref[rows, :] = di
            dx_s[rows, :] += out

        @pl.when(i == steps - 1)
        def _():
            out_b = gain_g = shift_g = 0.0
            for f in range(z.frames):
                rows = slice(f * FRAME_PAD, (f + 1) * FRAME_PAD)
                g2, gg, sg = norm_rows_back(h2_ref[f], gain_ref[2:3], dx_s[rows, :], g_ref[f])
                g2_ref[f] = g2
                spread[f * z.span : f * z.span + FRAME_PAD, :] = g2
                gain_g, shift_g = gain_g + gg, shift_g + sg
                out_b = out_b + jnp.sum(g2, axis=0, keepdims=True)
            sums_ref[1:2] = gain_g
            sums_ref[2:3] = shift_g
            sums_ref[3:4] = out_b
            send_pieces(z, place_ref, spread, piece_refs)

    frame = (z.frames, FRAME_PAD, D)
    piece = (z.groups, z.piece, D)
    step = pl.BlockSpec((z.rows, CHUNK), lambda i: (0, i))
    return call(
        body,
        "hidden_backward",
        (steps,),
        [SMEM, whole(frame), whole(frame), step]
        + [wu.step(CHUNK), wd.step(CHUNK), whole(gains.shape)],
        [step, whole((z.rows, D)), whole(frame), whole((4, D))] + [whole(piece)] * z.members,
        [
            shaped((z.rows, FF), BF),
            shaped((z.rows, D), BF),
            shaped(frame, F32),
            shaped((4, D), F32),
        ]
        + [shaped(piece, BF)] * z.members,
        [
            pltpu.VMEM((z.rows, D), F32),
            pltpu.VMEM((z.frames * z.span, D), F32),
        ],
        (place, grad, h2, slope, *wu.arrays, *wd.arrays, gains),
        2 * z.rows * D * 2 * FF,
    )


def temporal_backward(z, grad_pieces, qkv, wq, wo):
    wide = 3 * z.half
    n = z.group_rows

    def body(*refs):
        in_refs, refs = refs[: z.members], refs[z.members :]
        qkv_ref, *refs = refs
        wq_refs, refs = refs[: len(wq.arrays)], refs[len(wq.arrays) :]
        wo_refs, refs = refs[: len(wo.arrays)], refs[len(wo.arrays) :]
        d_ref, *refs = refs
        out_refs, refs = refs[: z.members], refs[z.members :]
        wq_s, wo_s, gb_s, dm_s, d_s, sem = refs
        g = pl.program_id(0)

        @pl.when(g == 0)
        def _():
            first = wo.copies(wo_refs, wo_s, sem.at[0])
            start_all(first)
            start_all(wq.copies(wq_refs, wq_s, sem.at[1]))
            gather_groups(z, in_refs, gb_s)
            wait_all(first)
            gb = gb_s[...]
            for c in range(z.cols):
                dm_s[:, c * z.half : (c + 1) * z.half] = dot_nn(gb, wo_s[c]).astype(BF)

        rows = pl.ds(pl.multiple_of(g * n, n), n)
        q, k, v = [[qkv_ref[0, :, at[t]] for at in pair_columns(z)] for t in range(3)]
        dm = [dm_s[rows, at[3]] for at in pair_columns(z)]
        grads = attend_all_back(q, k, v, dm, patch_valid(n))
        for at, values in zip(pair_columns(z), grads):
            for t in range(3):
                d_s[rows, at[t]] = values[t]
        d_ref[...] = d_s[rows, :]

        @pl.when(g == z.groups - 1)
        def _():
            wait_all(wq.copies(wq_refs, wq_s, sem.at[1]))
            dx = 0.0
            for c in range(z.cols):
                dx = dx + dot_nt(d_s[:, c * wide : (c + 1) * wide], wq_s[c])
            dx = dx.astype(BF)
            for gg in range(z.groups):
                for m in range(z.members):
                    at = gg * n + m * z.piece
                    out_refs[m][gg] = dx[at : at + z.piece]

    piece = (z.groups, z.piece, D)
    return call(
        body,
        "temporal_backward",
        (z.groups,),
        [whole(piece)] * z.members
        + [pl.BlockSpec((1, n, 3 * D), lambda g: (g, 0, 0))]
        + [HBM] * (len(wq.arrays) + len(wo.arrays)),
        [pl.BlockSpec((n, 3 * D), lambda g: (g, 0))] + [whole(piece)] * z.members,
        [shaped((z.patch_rows, 3 * D), BF)] + [shaped(piece, BF)] * z.members,
        [
            wq.scratch(),
            wo.scratch(),
            pltpu.VMEM((z.patch_rows, D), BF),
            pltpu.VMEM((z.patch_rows, D), BF),
            pltpu.VMEM((z.patch_rows, 3 * D), BF),
            pltpu.SemaphoreType.DMA((2,)),
        ],
        (*grad_pieces, qkv, *wq.arrays, *wo.arrays),
        2 * z.patch_rows * D * (4 * D + 5 * n),
    )


def spatial_backward(z, place, dx_pieces, grad, h1, qkv, wo, gains):
    wide = 3 * z.half

    def body(place_ref, *refs):
        in_refs, refs = refs[: z.members], refs[z.members :]
        g_ref, h1_ref, qkv_ref, *refs = refs
        wo_refs, refs = refs[: len(wo.arrays)], refs[len(wo.arrays) :]
        gain_ref, gb_ref, d_ref, g1_ref, sums_ref, *refs = refs
        wo_s, spread, dm_s, sem = refs
        f = pl.program_id(0)

        @pl.when(f == 0)
        def _():
            first = wo.copies(wo_refs, wo_s, sem.at[0])
            start_all(first)
            for m in range(z.members):
                rows = in_refs[m][...].reshape(z.groups * z.piece, D).astype(F32)
                take_pieces(z, place_ref, spread, m, rows)
            out_b = gain_g = shift_g = 0.0
            for at in range(z.frames):
                rows = slice(at * FRAME_PAD, (at + 1) * FRAME_PAD)
                dx = spread[at * z.span : at * z.span + FRAME_PAD, :]
                g1, gg, sg = norm_rows_back(h1_ref[at], gain_ref[1:2], dx, g_ref[at])
                g1_ref[at] = g1
                gb_ref[rows, :] = g1.astype(BF)
                gain_g, shift_g = gain_g + gg, shift_g + sg
                out_b = out_b + jnp.sum(g1, axis=0, keepdims=True)
            sums_ref[0:1] = gain_g
            sums_ref[1:2] = shift_g
            sums_ref[2:3] = out_b
            wait_all(first)
            gb = gb_ref[...]
            for c in range(z.cols):
                dm_s[:, c * z.half : (c + 1) * z.half] = dot_nn(gb, wo_s[c]).astype(BF)

        rows = pl.ds(pl.multiple_of(f * FRAME_PAD, 16), FRAME_PAD)
        q, k, v = [[qkv_ref[0, :, at[t]] for at in pair_columns(z)] for t in range(3)]
        dm = [dm_s[rows, at[3]] for at in pair_columns(z)]
        grads = attend_all_back(
            q, [key_rows(x) for x in k], [key_rows(x) for x in v], dm, frame_valid()
        )
        for at, values in zip(pair_columns(z), grads):
            for t in range(3):
                d_ref[:, at[t]] = values[t][:FRAME_PAD]

    frame = (z.frames, FRAME_PAD, D)
    piece = (z.groups, z.piece, D)
    return call(
        body,
        "spatial_backward",
        (z.frames,),
        [SMEM]
        + [whole(piece)] * z.members
        + [whole(frame), whole(frame), pl.BlockSpec((1, FRAME_PAD, 3 * D), lambda f: (f, 0, 0))]
        + [HBM] * len(wo.arrays)
        + [whole(gains.shape)],
        [
            whole((z.rows, D)),
            pl.BlockSpec((FRAME_PAD, 3 * D), lambda f: (f, 0)),
            whole(frame),
            whole((3, D)),
        ],
        [
            shaped((z.rows, D), BF),
            shaped((z.rows, 3 * D), BF),
            shaped(frame, F32),
            shaped((3, D), F32),
        ],
        [
            wo.scratch(),
            pltpu.VMEM((z.frames * z.span, D), F32),
            pltpu.VMEM((z.rows, D), BF),
            pltpu.SemaphoreType.DMA((1,)),
        ],
        (place, *dx_pieces, grad, h1, qkv, *wo.arrays, gains),
        2 * z.rows * D * (D + 5 * KEY_PAD),
    )


def input_backward(z, d, grad, hidden, wq, gains):
    wide = 3 * z.half

    def body(d_ref, g_ref, h_ref, *refs):
        wq_refs, refs = refs[: len(wq.arrays)], refs[len(wq.arrays) :]
        gain_ref, g0_ref, sums_ref, wq_s, sem = refs
        f = pl.program_id(0)

        @pl.when(f == 0)
        def _():
            copies = wq.copies(wq_refs, wq_s, sem.at[0])
            start_all(copies)
            wait_all(copies)
            sums_ref[...] = jnp.zeros_like(sums_ref)

        dx = 0.0
        for c in range(z.cols):
            dx = dx + dot_nt(d_ref[:, c * wide : (c + 1) * wide], wq_s[c])
        for at in range(2):
            rows = slice(at * FRAME_PAD, (at + 1) * FRAME_PAD)
            g0, gg, sg = norm_rows_back(h_ref[at], gain_ref[0:1], dx[rows], g_ref[at])
            g0_ref[at] = g0
            sums_ref[0:1] += gg
            sums_ref[1:2] += sg

    frame = (z.frames, FRAME_PAD, D)
    step = pl.BlockSpec((2, FRAME_PAD, D), lambda f: (f, 0, 0))
    return call(
        body,
        "input_backward",
        (z.frames // 2,),
        [pl.BlockSpec((2 * FRAME_PAD, 3 * D), lambda f: (f, 0)), step, step]
        + [HBM] * len(wq.arrays)
        + [whole(gains.shape)],
        [step, whole((2, D))],
        [shaped(frame, F32), shaped((2, D), F32)],
        [wq.scratch(), pltpu.SemaphoreType.DMA((1,))],
        (d, grad, hidden, *wq.arrays, gains),
        2 * z.rows * D * 3 * D,
    )


def weight_grads(z, place, name, jobs, direct, room=0, into=None, start_at=0):
    halves_ = [job[1][0].shape[-1] // z.cols for job in jobs]
    width = sum(halves_)
    even = len(set(halves_)) == 1
    starts = [sum(halves_[:k]) for k in range(len(jobs))]
    total = jobs[0][1][0].shape[-1]
    rows = [sum(a.shape[0] for a in job[0]) for job in jobs]
    outs = 2 if direct else 1

    def joined(refs):
        parts = [r[...] for r in refs]
        return parts[0] if len(parts) == 1 else jnp.concatenate(parts, 0)

    def body(place_ref, *refs):
        lefts, rights = [], []
        refs = refs[0 if into is None else 1 :]
        for left, right in jobs:
            lefts.append(refs[: len(left)])
            rights.append(refs[len(left) : len(left) + len(right)])
            refs = refs[len(left) + len(right) :]
        out_refs, sums_ref, turned = refs[:outs], refs[outs], refs[outs + 1 :]
        r, i = pl.program_id(0), pl.program_id(1)

        for k in range(len(jobs)):

            @pl.when(i == k)
            def _(k=k):
                @pl.when(r == 0)
                def _():
                    turned[k][...] = joined(lefts[k]).T

                value = joined(rights[k])
                if k == 0:
                    sums_ref[...] = jnp.sum(value.astype(F32), axis=0, keepdims=True)
                out = dot_nn(turned[k][...], value).astype(BF)
                start = 0 if even else starts[k]
                cut = slice(start, start + halves_[k])
                if not direct:
                    out_refs[0][0, :, cut] = out
                    return
                core = place_ref[3]
                for zz in range(z.depth):
                    for xx in range(2):
                        at = [z.block * ((zz * 2 + cc) * 2 + xx) for cc in range(2)]
                        first, second = [out[a : a + z.block] for a in at]
                        x, depth = xx ^ place_ref[1], zz ^ place_ref[4]
                        out_refs[0][0, x, depth, :, cut] = jnp.where(core == 0, first, second)
                        out_refs[1][0, x, depth, :, cut] = jnp.where(core == 0, second, first)

    def right_spec(k, a):
        def index(r, i, place_ref):
            return (0, r ^ place_ref[2] if direct else r)

        return pl.BlockSpec((a.shape[0], halves_[k]), index)

    in_specs, args = ([], []) if into is None else ([HBM], [into])
    for k, (left, right) in enumerate(jobs):
        in_specs += [whole(a.shape) for a in left] + [right_spec(k, a) for a in right]
        args += [*left, *right]
    block = halves_[0] if even else width
    first = start_at // block
    if direct:
        part = (2, z.depth, z.block)
        out_specs = [
            pl.BlockSpec((1,) + part + (block,), lambda r, i, p: (r, 0, 0, 0, i if even else 0))
        ] * 2
        out_shape = [shaped((z.cols,) + part + (width,), BF)] * 2
    else:
        out_specs = [pl.BlockSpec((1, D, block), lambda r, i, p: (r, 0, first + (i if even else 0)))]
        out_shape = [shaped((z.cols, D, width + room) if into is None else into.shape, BF)]
    out_specs.append(right_spec(0, shaped((1, total), F32)))
    out_shape.append(shaped((1, total), F32))
    flops = sum(2 * n * D * h * z.cols for n, h in zip(rows, halves_))
    moved = sum(a.size * a.dtype.itemsize for a in args + out_shape)
    scratch = [pltpu.VMEM((D, n), BF) for n in rows]
    limit = vmem_bytes([*in_specs, *out_specs], [*args, *out_shape], scratch)
    *parts, sums = pl.pallas_call(
        body,
        name=name,
        grid_spec=pltpu.PrefetchScalarGridSpec(
            num_scalar_prefetch=1,
            grid=(z.cols, len(jobs)),
            in_specs=in_specs,
            out_specs=out_specs,
            scratch_shapes=scratch,
        ),
        out_shape=out_shape,
        input_output_aliases={} if into is None else {1: 0},
        compiler_params=pltpu.CompilerParams(
            vmem_limit_bytes=limit, dimension_semantics=("arbitrary",) * 2
        ),
        cost_estimate=pl.CostEstimate(flops=int(flops), bytes_accessed=int(moved), transcendentals=0),
    )(place, *args)
    return parts, sums


def swap(value, axis, apart):
    pairs = [(at, at ^ apart) for at in range(lax.axis_size(axis))]
    return lax.ppermute(value, axis, pairs)


def add_terms(terms):
    total = terms[0].astype(F32)
    for term in terms[1:]:
        total = total + term.astype(F32)
    return total


def add_low(terms):
    return add_terms(terms).astype(BF)


def reduce_whole(z, part):
    flat_rows = part.reshape(z.cols * D, -1)
    own = lax.psum_scatter(flat_rows, ROWS_AXES, scatter_dimension=0, tiled=True)
    return own.astype(F32)


def reduce_steps(z, keep, send):
    (got,) = yield [(send, "dp", 1)]
    terms = [keep, got]
    half = z.depth // 2

    def of(*at):
        return [term[at] for term in terms]

    low, high = slice(0, half), slice(half, None)
    over_x, over_y = yield [
        (add_low(of(slice(None), 1, low)), "row", 1),
        (add_low(of(1, slice(None), high)), "col", 1),
    ]
    x_high, y_low = yield [
        (add_low(of(0, 1, high) + [over_y[1]]), "row", 1),
        (add_low(of(1, 0, low) + [over_x[1]]), "col", 1),
    ]
    lows = of(0, 0, low) + [over_x[0], y_low]
    highs = of(0, 0, high) + [x_high, over_y[0]]
    apart = z.depth
    while True:
        (got,) = yield [(add_low(highs), "dp", apart)]
        lows = lows + [got]
        if half == 1:
            return add_terms([term[0] for term in lows])
        half //= 2
        apart //= 2
        highs = [term[half:] for term in lows]
        lows = [term[:half] for term in lows]


class Mover:
    def __init__(self):
        self.flying = []

    def launch(self, value, started):
        moves = [list(next_moves) for _, next_moves, _ in started]
        operands = [[move[0] for move in group] for group in moves]
        value, operands = lax.optimization_barrier((value, operands))
        for (steps, _, done), group, held in zip(started, moves, operands):
            arrived = [swap(v, axis, apart) for v, (_, axis, apart) in zip(held, group)]
            self.flying.append((steps, arrived, done))
        return value

    def add(self, value, steps, done):
        return self.launch(value, [(steps, next(steps), done)])

    def tick(self, value):
        flying, self.flying = self.flying, []
        if not flying:
            return value
        value, landed = lax.optimization_barrier((value, [f[1] for f in flying]))
        started = []
        for (steps, _, done), arrived in zip(flying, landed):
            try:
                started.append((steps, steps.send(arrived), done))
            except StopIteration as stop:
                done(stop.value)
        return self.launch(value, started) if started else value


def sum_everywhere(value):
    for axis in ALL_AXES:
        apart = 1
        while apart < lax.axis_size(axis):
            value = value + swap(value, axis, apart)
            apart *= 2
    return value


def clip_swap(value, apart):
    count = lax.axis_size("row") * lax.axis_size("col")
    return lax.ppermute(value, CLIP_AXES, [(at, at ^ apart) for at in range(count)])


def swap_pieces(pieces):
    return [pieces[0]] + [clip_swap(pieces[apart], apart) for apart in range(1, len(pieces))]


def flat(pieces):
    return [p.reshape(-1, D) for p in pieces]


def pad_frames(z, rows):
    grid = rows.reshape(z.frames, PATCHES, D)
    return jnp.pad(grid, ((0, 0), (0, FRAME_PAD - PATCHES), (0, 0)))


def cut_frames(z, grid):
    return grid[:, :PATCHES].reshape(z.frames * PATCHES, D)


def layer_forward(z, place, hidden, w, small):
    gains, shifts, bias_qkv, bias_out, bias_up, bias_down = small
    x0, qkv0, mixed0, h1, *send = spatial_forward(
        z, place, hidden, w["qkv0"], w["out0"], bias_qkv[0], bias_out, gains, shifts
    )
    pieces = swap_pieces(send)
    qkv1, *back = temporal_forward(z, pieces, w["qkv1"], bias_qkv[1])
    mixed1 = swap_pieces(back)
    h2, x2, act, slope, h3 = hidden_forward(
        z, place, mixed1, h1, w["out1"], w["up"], w["down"], bias_out, bias_up, bias_down, gains, shifts
    )
    return h3, (hidden, x0, qkv0, mixed0, h1, pieces, qkv1, mixed1, h2, x2, act, slope)


def group_rows(z, pieces):
    stacked = jnp.stack(pieces, axis=1)
    return stacked.reshape(z.patch_rows, D)


def partial_set(owned, name):
    return lambda value: owned.__setitem__(name, value)


def after(value, other):
    return lax.optimization_barrier((value, other))[0]


def layer_backward(z, place, grad, record, w, small, owned, mover, direct, carry):
    gains, *_ = small
    hidden, x0, qkv0, mixed0, h1, pieces, qkv1, mixed1, h2, x2, act, slope = record
    di, gb, g2, sums_h, *send = hidden_backward(z, place, grad, h2, slope, w["up"], w["down"], gains)
    got = swap_pieces(send)
    jobs = [([x2], [di]), ([gb], [act])]
    part = 4 * z.half
    if carry is None:
        parts, up_b = weight_grads(z, place, "hidden_grads", jobs, False)
        owned["hidden"] = reduce_whole(z, parts[0])
    else:
        parts, up_b = weight_grads(
            z, place, "hidden_grads", jobs, False, into=carry[0], start_at=2 * part
        )
        whole_rows = reduce_whole(z, parts[0])
        carry[1]["temporal"] = whole_rows[:, :part]
        carry[1]["spatial"] = whole_rows[:, part : 2 * part]
        owned["hidden"] = whole_rows[:, 2 * part :]
    got[0] = after(got[0], up_b)
    d1, *back = temporal_backward(z, got, qkv1, w["qkv1"], w["out1"])
    dx = swap_pieces(back)
    jobs = [([group_rows(z, pieces)], [d1]), (flat(send), flat(mixed1))]
    room = 0 if direct else part + 2 * z.units
    parts, qkv1_b = weight_grads(z, place, "temporal_grads", jobs, direct, room)
    dx[0] = after(dx[0], qkv1_b)
    if direct:
        g2 = mover.add(g2, reduce_steps(z, *parts), partial_set(owned, "temporal"))
    gb, d0, g1, sums_s = spatial_backward(z, place, dx, g2, h1, qkv0, w["out0"], gains)
    jobs = [([x0.reshape(z.rows, D)], [d0]), ([gb], [mixed0.reshape(z.rows, D)])]
    if direct:
        d0 = mover.tick(d0)
        jobs[0] = (jobs[0][0], [d0])
        parts, qkv0_b = weight_grads(z, place, "spatial_grads", jobs, True)
        g1 = mover.tick(g1)
        g1 = mover.add(g1, reduce_steps(z, *parts), partial_set(owned, "spatial"))
    else:
        parts, qkv0_b = weight_grads(
            z, place, "spatial_grads", jobs, False, into=parts[0], start_at=part
        )
    g0, sums_i = input_backward(z, d0, g1, hidden, w["qkv0"], gains)

    def qv(sums):
        parts = sums.reshape(z.cols, 3, z.half)
        return jnp.stack([parts[:, 0].reshape(D), parts[:, 2].reshape(D)])

    gain = jnp.stack([sums_i[0], sums_s[0], sums_h[1]])
    shift = jnp.stack([sums_i[1], sums_s[1], sums_h[2]])
    qv_g = jnp.concatenate([qv(qkv0_b), qv(qkv1_b)])
    out_g = jnp.stack([sums_s[2], sums_h[3]])
    small_g = jnp.concatenate([gain, shift, qv_g, out_g, sums_h[0:1], up_b.reshape(-1, D)])
    return g0, small_g, (parts[0], owned)


def own_parts(qkv_weight, out_weight, up_weight, down_weight, at):
    rows = up_weight.shape[1]
    return {
        "qkv0": qkv_weight[at, 0].reshape(rows, -1),
        "out0": out_weight[at, 0].T,
        "qkv1": qkv_weight[at, 1].reshape(rows, -1),
        "out1": out_weight[at, 1].T,
        "up": up_weight[at],
        "down": down_weight[at].T,
    }


ATTENTION_PARTS = ("qkv0", "qkv1", "out0", "out1")
HIDDEN_PARTS = ("up", "down")


def fetch(parts, cols, batches):
    result = {}
    for names in batches:
        packed = jnp.concatenate([parts[name] for name in names], axis=1)
        full = lax.all_gather(packed, ROWS_AXES, axis=0, tiled=True).reshape(cols, D, -1)
        at = 0
        for name in names:
            width = parts[name].shape[1]
            result[name] = Weight(full, at, width)
            at += width
    return result


def over_cols(value):
    if lax.axis_size("col") != 2:
        return lax.all_gather(value, "col", axis=0)
    other = swap(value, "col", 1)
    first = lax.axis_index("col") == 0
    return jnp.where(first, jnp.stack([value, other]), jnp.stack([other, value]))


def shards(
    hidden_in,
    qkv_weight,
    out_weight,
    up_weight,
    down_weight,
    qv_bias,
    out_bias,
    up_bias,
    down_bias,
    norm_gain,
    norm_shift,
    cotangent,
):
    layers = qkv_weight.shape[0]
    cols = lax.axis_size("col")
    z = Sizes(
        hidden_in.shape[0], up_weight.shape[1], lax.axis_size("dp") // 2, lax.axis_size("row"), cols
    )
    row_at, col_at, dp_at = lax.axis_index("row"), lax.axis_index("col"), lax.axis_index("dp")
    place = [(row_at * cols + col_at) % z.members, row_at, col_at, dp_at % 2, dp_at // 2]
    place = jnp.stack(place).astype(jnp.int32)
    biases = over_cols(jnp.concatenate([qv_bias.reshape(layers, -1), up_bias], axis=1))
    qv_all = biases[:, :, : 4 * z.half].reshape(cols, layers, 2, 2, 1, z.half)
    qv_all = jnp.moveaxis(qv_all, 0, 2)
    up_all = jnp.moveaxis(biases[:, :, 4 * z.half :], 0, 1).reshape(layers, FF)
    zero = jnp.zeros_like(qv_all[:, :, :, 0])
    bias_qkv = jnp.concatenate([qv_all[:, :, :, 0], zero, qv_all[:, :, :, 1]], axis=-1)
    hidden = pad_frames(z, hidden_in)
    kept = []
    for at in range(layers):
        parts = own_parts(qkv_weight, out_weight, up_weight, down_weight, at)
        batches = (ATTENTION_PARTS + HIDDEN_PARTS,) if at == 0 else (ATTENTION_PARTS, HIDDEN_PARTS)
        w = fetch(parts, cols, batches)
        small = (
            norm_gain[at],
            norm_shift[at],
            bias_qkv[at],
            out_bias[at],
            up_all[at][None],
            down_bias[at][None],
        )
        hidden, record = layer_forward(z, place, hidden, w, small)
        kept.append((w, small, record))
    grad = pad_frames(z, cotangent)
    owned = [{} for _ in range(layers)]
    smalls = [None] * layers
    mover, carry = Mover(), None
    for at in reversed(range(layers)):
        w, small, record = kept[at]
        direct = z.direct and at == 0
        grad, small_g, carry = layer_backward(
            z, place, grad, record, w, small, owned[at], mover, direct, carry
        )
        smalls[at] = sum_everywhere(small_g)
    if not z.direct:
        part = 4 * z.half
        last = reduce_whole(z, carry[0][:, :, : 2 * part])
        owned[0]["temporal"], owned[0]["spatial"] = last[:, :part], last[:, part:]
    while mover.flying:
        grad = mover.tick(grad)
    rows, units = z.block, z.units
    qkv_cols = 3 * z.half

    def attention_parts(make):
        return jnp.stack(
            [jnp.stack([make(o["spatial"]), make(o["temporal"])]) for o in owned]
        )

    grad_qkv = attention_parts(lambda a: a[:, :qkv_cols].reshape(rows, 3, z.half))
    grad_out = attention_parts(lambda a: a[:, qkv_cols:].T)
    grad_up = jnp.stack([o["hidden"][:, :units] for o in owned])
    grad_down = jnp.stack([o["hidden"][:, units:].T for o in owned])
    terms = jnp.stack(smalls)
    gain, shift = terms[:, 0:3], terms[:, 3:6]
    qv = terms[:, 6:10].reshape(layers, 2, 2, D)
    outb, downb, upb = terms[:, 10:12], terms[:, 12], terms[:, 13:].reshape(layers, FF)
    qv = lax.dynamic_slice_in_dim(qv, col_at * z.half, z.half, 3)
    upb = lax.dynamic_slice_in_dim(upb, col_at * z.units, z.units, 1)
    return (
        cut_frames(z, hidden),
        cut_frames(z, grad),
        grad_qkv,
        grad_out,
        grad_up,
        grad_down,
        qv,
        outb,
        upb,
        downb,
        gain,
        shift,
    )


def solution(mesh):
    return jax.shard_map(
        shards,
        mesh=mesh,
        in_specs=(
            P(("dp", "row", "col"), None),
            P(None, None, ("dp", "row"), None, "col"),
            P(None, None, "col", ("dp", "row")),
            P(None, ("dp", "row"), "col"),
            P(None, "col", ("dp", "row")),
            P(None, None, None, "col"),
            P(),
            P(None, "col"),
            P(),
            P(),
            P(),
            P(("dp", "row", "col"), None),
        ),
        out_specs=(
            P(("dp", "row", "col"), None),
            P(("dp", "row", "col"), None),
            P(None, None, ("dp", "row"), None, "col"),
            P(None, None, "col", ("dp", "row")),
            P(None, ("dp", "row"), "col"),
            P(None, "col", ("dp", "row")),
            P(None, None, None, "col"),
            P(),
            P(None, "col"),
            P(),
            P(),
            P(),
        ),
        check_vma=False,
    )
```
